512 devices in a mesh: chan: 16 (over y, core), tm: 32 (over z, x).
Axes of the slice: x: 4, y: 8, z: 8, core: 2. Of those that a mesh axis runs over, the one named last changes fastest.
Arguments:
- strain: bfloat16 [32, 64, 128, 1024], P('tm', 'chan'), may hold values from -60 to 60, as said below
- pair_slots: int32 [192, 2], P('chan'), may hold values from -1 to 63, as said below
Outputs:
- coherence: float32 [128, 192, 256], P('tm', 'chan')
The draws below stay inside these ranges and needn't reach their ends.
Inputs may be any that keep to these rules, and one draw needn't show every extreme that they name: `strain`: samples of one channel share a scale; values stay within the range. `pair_slots`: row s belongs to owner s // 12; a live slot holds blocks a <= b with b - a <= 8, both within 8 blocks of the owner's own blocks (owner o holds blocks o * 4 to o * 4 + 3); an empty slot holds -1, -1. Each owner's live slots come first and number 2 to 12; in every draw one owner fills all 12 slots and another holds 2.
All inputs are finite; a program needn't handle non-finite values.
Results may differ from the reference program's by a relative error of at most 0.00061.
Values may be sent and summed in bfloat16 or wider, within the bound.
No kernel may reach another device: no remote copies, remote signals or barrier semaphores. Data moves between devices by JAX's collectives and lax.ppermute only.
A program may use at most 128 MiB of HBM per device.

```python
import math
import jax
import jax.numpy as jnp
from jax import lax

CH = 128
SAMP = 1024
F = 1024
BLK_DEV = 4
CAP = 12
MAXOFF = 8
NBLK = 64
SLOTS = 192
SUBWIN = 32
N_CHAN = 16


def draw_strain(key, part):
    key = jax.random.fold_in(key, 11)
    key_rough, key_scale = jax.random.split(key, 2)
    dims_all = (SUBWIN, NBLK, CH, SAMP)
    scales = jnp.exp(jax.random.uniform(key_scale, (1, NBLK, CH, 1), jnp.float32, 0.0, math.log(10.0)))
    values = jnp.clip(jax.random.normal(key_rough, dims_all, jnp.float32), -5.0, 5.0) * scales
    return values.astype(jnp.bfloat16)


def draw_pair_slots(key, part):
    key = jax.random.fold_in(key, 23)
    key_first, key_offset, key_count, key_busy = jax.random.split(key, 4)
    owners = jnp.arange(N_CHAN, dtype=jnp.int32)
    owner_col = owners[:, None]
    lowest = jnp.maximum(owner_col * BLK_DEV - MAXOFF, 0)
    highest = jnp.minimum((owner_col + 1) * BLK_DEV - 1 + MAXOFF, NBLK - 1)
    span_size = highest - lowest + 1
    first_block = lowest + jax.random.randint(key_first, (N_CHAN, CAP), 0, 1 << 20, dtype=jnp.int32) % span_size
    offsets = jax.random.randint(key_offset, (N_CHAN, CAP), 0, MAXOFF + 1, dtype=jnp.int32)
    second_block = jnp.minimum(first_block + offsets, highest)
    slot_axis = jnp.arange(CAP, dtype=jnp.int32)[None, :]
    first_block = jnp.where(slot_axis == 0, lowest, first_block)
    second_block = jnp.where(slot_axis == 0, jnp.minimum(lowest + MAXOFF, highest), second_block)
    first_block = jnp.where(slot_axis == 1, jnp.maximum(highest - MAXOFF, lowest), first_block)
    second_block = jnp.where(slot_axis == 1, highest, second_block)
    drawn = jax.random.randint(key_count, (N_CHAN,), 0, CAP - 1, dtype=jnp.int32)
    counts = 2 + drawn * drawn // max(CAP - 2, 1)
    busiest = jax.random.randint(key_busy, (), 0, N_CHAN, dtype=jnp.int32)
    counts = jnp.where(owners == busiest, CAP, jnp.where(owners == (busiest + 1) % N_CHAN, 2, counts))
    active = slot_axis < counts[:, None]
    first_block = jnp.where(active, first_block, -1)
    second_block = jnp.where(active, second_block, -1)
    return jnp.stack([first_block, second_block], axis=-1).reshape(N_CHAN * CAP, 2).astype(jnp.int32)


def setup_inputs(seed: int = 0) -> dict:
    seeds = jax.random.split(jax.random.key(seed), 3)
    strain = draw_strain(jax.random.fold_in(seeds[2], 71), 0)
    pair_slots = draw_pair_slots(jax.random.fold_in(seeds[2], 71), 0)
    return dict(strain=strain, pair_slots=pair_slots)


def spectral_table(samples, bins):
    sample_axis = lax.iota(jnp.int32, samples)
    bin_axis = lax.iota(jnp.int32, bins) + 1
    phases = sample_axis[:, None] * bin_axis[None, :] % (2 * samples)
    angles = phases.astype(jnp.float32) * (math.pi / samples)
    tapers = 0.5 - 0.5 * jnp.cos(sample_axis.astype(jnp.float32) * (2.0 * math.pi / samples))
    whole = jnp.concatenate([jnp.cos(angles), -jnp.sin(angles)], axis=1) * tapers[:, None]
    return whole.astype(jnp.bfloat16)

def whiten(blocks, table_bf):
    block_count, channels, samples = blocks.shape
    bins = table_bf.shape[1] // 2
    spectra = jnp.dot(blocks.reshape(block_count * channels, samples), table_bf, preferred_element_type=jnp.float32)
    spectra = spectra.reshape(block_count, channels, 2 * bins)
    powers = spectra[:, :, :bins] * spectra[:, :, :bins] + spectra[:, :, bins:] * spectra[:, :, bins:]
    levels = jnp.sqrt(lax.optimization_barrier(jnp.mean(powers, axis=1)) + 1e-05)
    both_levels = jnp.concatenate([levels, levels], axis=1)
    return (spectra / both_levels[:, None, :]).astype(jnp.bfloat16)

def reference(strain, pair_slots):
    table_bf = spectral_table(SAMP, F)
    first_block = pair_slots[:, 0]
    second_block = pair_slots[:, 1]
    active = first_block >= 0
    index_a = jnp.where(active, first_block, 0).astype(jnp.int32)
    index_b = jnp.where(active, second_block, 0).astype(jnp.int32)
    active_f = active.astype(jnp.float32)

    def one_window(running, block_set):
        whitened = whiten(block_set, table_bf)
        source = whitened[index_a].astype(jnp.float32)
        partner = whitened[index_b].astype(jnp.float32)
        turned = jnp.concatenate([-partner[:, :, F:], partner[:, :, :F]], axis=2)
        stacked_partner = jnp.concatenate([partner, turned], axis=1)
        term = jnp.einsum('sif,sjf->sij', source, stacked_partner)
        return (running + term * active_f[:, None, None], None)
    start_total = jnp.zeros((SLOTS, CH, 2 * CH), jnp.float32)
    running, _ = lax.scan(one_window, start_total, strain)
    return jnp.transpose(running, (1, 0, 2)) / (F * SUBWIN)
```

```python
import functools
import math

import jax
import jax.numpy as jnp
from jax import lax
from jax.experimental import pallas as pl
from jax.experimental.pallas import tpu as pltpu
from jax.sharding import PartitionSpec as P

LANES = 128
CHUNK = 256
ROWS_PERIOD = 16
GROUPS = 5
VMEM = 24 * 1024 * 1024


def table_parts(samples):
    sample = lax.broadcasted_iota(jnp.int32, (samples, LANES), 0)
    low = lax.broadcasted_iota(jnp.int32, (samples, LANES), 1) + 1
    angles = (sample * low % (2 * samples)).astype(jnp.float32) * (math.pi / samples)
    tapers = 0.5 - 0.5 * jnp.cos(sample.astype(jnp.float32) * (2.0 * math.pi / samples))
    steps = samples // LANES
    period = 2 * samples // LANES
    shape = (steps, period, LANES)
    step = lax.broadcasted_iota(jnp.int32, shape, 0)
    row = lax.broadcasted_iota(jnp.int32, shape, 1)
    turns = (step * row % period).astype(jnp.float32) * (2.0 * math.pi / period)
    return tapers * jnp.cos(angles), tapers * jnp.sin(angles), jnp.cos(turns), jnp.sin(turns)


def whiten_chunk(x, table, out_ref):
    blocks, channels, samples = x.shape
    spectra = jnp.dot(x.reshape(blocks * channels, samples), table, preferred_element_type=jnp.float32)
    for block in range(blocks):
        part = spectra[block * channels : (block + 1) * channels]
        real, imag = part[:, :CHUNK], part[:, CHUNK:]
        power = jnp.sum(real * real + imag * imag, axis=0, keepdims=True) * (1.0 / channels)
        scale = 1.0 / jnp.sqrt(power + 1e-05)
        out_ref[block, :channels, :] = (real * scale).astype(jnp.bfloat16)
        out_ref[block, channels:, :] = (imag * scale).astype(jnp.bfloat16)


def first_kernel(cos_ref, sin_ref, step_cos_ref, step_sin_ref, x_ref, table_ref, out_ref):
    chunk = pl.program_id(0)
    samples = x_ref.shape[2]
    period = step_cos_ref.shape[1]
    shape = (samples // period, period, LANES)
    low_cos = cos_ref[...].reshape(shape)
    low_sin = sin_ref[...].reshape(shape)
    per_chunk = CHUNK // LANES
    for part in range(per_chunk):
        step_cos = step_cos_ref[chunk * per_chunk + part][None]
        step_sin = step_sin_ref[chunk * per_chunk + part][None]
        real = low_cos * step_cos - low_sin * step_sin
        imag = -(low_sin * step_cos + low_cos * step_sin)
        columns = slice(part * LANES, (part + 1) * LANES)
        table_ref[:, columns] = real.reshape(samples, LANES).astype(jnp.bfloat16)
        columns = slice(CHUNK + part * LANES, CHUNK + (part + 1) * LANES)
        table_ref[:, columns] = imag.reshape(samples, LANES).astype(jnp.bfloat16)
    whiten_chunk(x_ref[...], table_ref[...], out_ref)


def whiten_first(x, parts):
    blocks, channels, samples = x.shape
    cos, sin, step_cos, step_sin = parts
    whole = lambda a: pl.BlockSpec(a.shape, lambda j: (0,) * a.ndim)
    return pl.pallas_call(
        first_kernel,
        grid=(samples // CHUNK,),
        in_specs=[whole(cos), whole(sin), whole(step_cos), whole(step_sin), whole(x)],
        out_specs=[
            pl.BlockSpec((samples, 2 * CHUNK), lambda j: (0, j)),
            pl.BlockSpec((blocks, 2 * channels, CHUNK), lambda j: (0, 0, j)),
        ],
        out_shape=[
            jax.ShapeDtypeStruct((samples, 2 * samples), jnp.bfloat16),
            jax.ShapeDtypeStruct((GROUPS * blocks, 2 * channels, samples), jnp.bfloat16),
        ],
        compiler_params=pltpu.CompilerParams(vmem_limit_bytes=VMEM),
        cost_estimate=pl.CostEstimate(
            flops=4 * blocks * channels * samples * samples, bytes_accessed=8 << 20, transcendentals=0
        ),
        name="table_and_own",
    )(cos, sin, step_cos, step_sin, x)


def next_kernel(x_ref, table_ref, window_ref, out_ref):
    del window_ref
    whiten_chunk(x_ref[...], table_ref[...], out_ref)


def whiten_into(window, place, x, table, name):
    blocks, channels, samples = x.shape
    return pl.pallas_call(
        next_kernel,
        grid=(samples // CHUNK,),
        in_specs=[
            pl.BlockSpec(x.shape, lambda j: (0, 0, 0)),
            pl.BlockSpec((samples, 2 * CHUNK), lambda j: (0, j)),
            pl.BlockSpec(memory_space=pl.ANY),
        ],
        out_specs=pl.BlockSpec((blocks, 2 * channels, CHUNK), lambda j: (place, 0, j)),
        out_shape=jax.ShapeDtypeStruct(window.shape, window.dtype),
        input_output_aliases={2: 0},
        compiler_params=pltpu.CompilerParams(vmem_limit_bytes=VMEM),
        cost_estimate=pl.CostEstimate(
            flops=4 * blocks * channels * samples * samples, bytes_accessed=8 << 20, transcendentals=0
        ),
        name=name,
    )(x, table, window)


def pair_kernel(owner_ref, slots_ref, a0_ref, b0_ref, a1_ref, b1_ref, out_ref):
    del owner_ref
    step = pl.program_id(0)
    channels = a0_ref.shape[1] // 2
    found = []
    for a_ref, b_ref, slot in ((a0_ref, b0_ref, 2 * step), (a1_ref, b1_ref, 2 * step + 1)):
        product = lax.dot_general(
            a_ref[0], b_ref[0], (((1,), (1,)), ((), ())), preferred_element_type=jnp.float32
        )
        real = product[:channels, :channels] + product[channels:, channels:]
        imag = product[channels:, :channels] - product[:channels, channels:]
        live = jnp.where(slots_ref[2 * slot] >= 0, 0.25, 0.0)
        both = jnp.concatenate([real, imag], axis=1) * live
        found.append(both.reshape(channels // 8, 8, 2 * channels))
    first, second = found
    row = lax.broadcasted_iota(jnp.int32, first.shape, 1)
    out_ref[:, 0] = jnp.where(row < 4, first, pltpu.roll(second, 4, 1))
    out_ref[:, 1] = jnp.where(row < 4, pltpu.roll(first, 4, 1), second)


def pair_products(window, slots, owner, own_blocks):
    _, stacked, samples = window.shape
    channels = stacked // 2
    slot_count = slots.shape[0]

    def place(owner_ref, slots_ref, entry):
        owner = owner_ref[0]
        block = slots_ref[entry]
        block = jnp.where(block >= 0, block, owner * own_blocks)
        side = 1 - 2 * lax.rem(owner, 2)
        away = (lax.div(block, own_blocks) - owner) * side
        return lax.rem(away + GROUPS, GROUPS) * own_blocks + lax.rem(block, own_blocks)

    def spec(which):
        return pl.BlockSpec(
            (1, stacked, samples),
            lambda i, owner_ref, slots_ref: (place(owner_ref, slots_ref, 4 * i + which), 0, 0),
        )

    return pl.pallas_call(
        pair_kernel,
        grid_spec=pltpu.PrefetchScalarGridSpec(
            num_scalar_prefetch=2,
            grid=(slot_count // 2,),
            in_specs=[spec(0), spec(1), spec(2), spec(3)],
            out_specs=pl.BlockSpec((channels // 8, 2, 8, 2 * channels), lambda i, *_: (0, 0, i, 0)),
        ),
        out_shape=jax.ShapeDtypeStruct((channels // 8, 2, slot_count * 4, 2 * channels), jnp.float32),
        compiler_params=pltpu.CompilerParams(vmem_limit_bytes=VMEM),
        cost_estimate=pl.CostEstimate(
            flops=slot_count * 8 * channels * channels * samples, bytes_accessed=14 << 20, transcendentals=0
        ),
        name="pair_products",
    )(owner, slots.reshape(-1), window, window, window, window)


def on_device(strain, pair_slots):
    x = strain[0]
    blocks, channels, samples = x.shape
    owners = lax.axis_size("chan")
    windows = lax.axis_size("tm")
    slot_count = pair_slots.shape[0]
    owner = lax.axis_index("chan")
    even = range(0, owners, 2)
    odd = range(1, owners, 2)
    sibling_pairs = [(i, i ^ 1) for i in range(owners)]
    near_pairs = [((i + 2) % owners, i) for i in even] + [((i - 2) % owners, i) for i in odd]
    far_pairs = [((i - 2) % owners, i) for i in even] + [((i + 2) % owners, i) for i in odd]

    passed_on = lax.ppermute(x, "chan", near_pairs)
    sibling = lax.ppermute(x, "chan", sibling_pairs)
    far = lax.ppermute(x, "chan", far_pairs)
    table, window = whiten_first(x, table_parts(samples))
    window = whiten_into(window, 1, sibling, table, "sibling")
    from_sibling = lax.ppermute(passed_on, "chan", sibling_pairs)
    window = whiten_into(window, 2, passed_on, table, "near")
    window = whiten_into(window, 4, from_sibling, table, "passed")
    window = whiten_into(window, 3, far, table, "far")

    products = pair_products(window, pair_slots, owner.reshape(1), blocks)
    rows = channels // windows
    products = products.reshape(windows, slot_count * rows, 2 * channels).astype(jnp.float16)
    arrived = lax.all_to_all(products, "tm", 0, 0, tiled=True)
    total = jnp.sum(arrived.astype(jnp.float32), axis=0) * (4.0 / (samples * windows))
    return jnp.transpose(total.reshape(slot_count, rows, 2 * channels), (1, 0, 2))


def solution(mesh):
    return jax.shard_map(
        on_device,
        mesh=mesh,
        in_specs=(P("tm", "chan", None, None), P("chan", None)),
        out_specs=P("tm", "chan", None),
        check_vma=False,
    )
```

```python
import functools
import math

import jax
import jax.numpy as jnp
from jax import lax
from jax.experimental import pallas as pl
from jax.experimental.pallas import tpu as pltpu
from jax.sharding import PartitionSpec as P

LANES = 128
CHUNK = 256
ROWS_PERIOD = 16
SPLIT = 32
GROUPS = 5
VMEM = 24 * 1024 * 1024


def table_parts(samples):
    shape = (4 * SPLIT + samples // LANES * ROWS_PERIOD, LANES)
    row = lax.broadcasted_iota(jnp.int32, shape, 0)
    bin_low = lax.broadcasted_iota(jnp.int32, shape, 1) + 1
    part = row // SPLIT
    at = row % SPLIT
    step_row = row - 4 * SPLIT
    phases = jnp.where(
        part == 0,
        bin_low * at * SPLIT,
        jnp.where(
            part == 1,
            bin_low * at,
            jnp.where(
                part == 2,
                2 * SPLIT * at,
                jnp.where(part == 3, 2 * at, (step_row // ROWS_PERIOD) * (step_row % ROWS_PERIOD) * LANES),
            ),
        ),
    )
    angles = (phases % (2 * samples)).astype(jnp.float32) * (math.pi / samples)
    return jnp.cos(angles), jnp.sin(angles)


def whiten_chunk(x, table, out_ref):
    blocks, channels, samples = x.shape
    spectra = jnp.dot(x.reshape(blocks * channels, samples), table, preferred_element_type=jnp.float32)
    for block in range(blocks):
        part = spectra[block * channels : (block + 1) * channels]
        real, imag = part[:, :CHUNK], part[:, CHUNK:]
        power = jnp.sum(real * real + imag * imag, axis=0, keepdims=True) * (1.0 / channels)
        scale = 1.0 / jnp.sqrt(power + 1e-05)
        out_ref[block, :channels, :] = (real * scale).astype(jnp.bfloat16)
        out_ref[block, channels:, :] = (imag * scale).astype(jnp.bfloat16)


def first_kernel(cos_ref, sin_ref, x_ref, table_ref, out_ref, low_cos_ref, low_sin_ref):
    chunk = pl.program_id(0)
    samples = x_ref.shape[2]

    @pl.when(chunk == 0)
    def _():
        rows = lambda ref, part: ref[part * SPLIT : (part + 1) * SPLIT, :]
        for at in range(samples // SPLIT):
            high = lambda ref, part: ref[part * SPLIT + at : part * SPLIT + at + 1, :]
            taper = 0.5 - 0.5 * (
                high(cos_ref, 2) * rows(cos_ref, 3) - high(sin_ref, 2) * rows(sin_ref, 3)
            )
            cos = high(cos_ref, 0) * rows(cos_ref, 1) - high(sin_ref, 0) * rows(sin_ref, 1)
            sin = high(sin_ref, 0) * rows(cos_ref, 1) + high(cos_ref, 0) * rows(sin_ref, 1)
            low_cos_ref[at * SPLIT : (at + 1) * SPLIT, :] = taper * cos
            low_sin_ref[at * SPLIT : (at + 1) * SPLIT, :] = taper * sin

    shape = (samples // ROWS_PERIOD, ROWS_PERIOD, LANES)
    low_cos = low_cos_ref[...].reshape(shape)
    low_sin = low_sin_ref[...].reshape(shape)
    per_chunk = CHUNK // LANES
    for part in range(per_chunk):
        first_row = 4 * SPLIT + (chunk * per_chunk + part) * ROWS_PERIOD
        step_rows = pl.ds(pl.multiple_of(first_row, ROWS_PERIOD), ROWS_PERIOD)
        step_cos = cos_ref[step_rows, :][None]
        step_sin = sin_ref[step_rows, :][None]
        real = low_cos * step_cos - low_sin * step_sin
        imag = -(low_sin * step_cos + low_cos * step_sin)
        columns = slice(part * LANES, (part + 1) * LANES)
        table_ref[:, columns] = real.reshape(samples, LANES).astype(jnp.bfloat16)
        columns = slice(CHUNK + part * LANES, CHUNK + (part + 1) * LANES)
        table_ref[:, columns] = imag.reshape(samples, LANES).astype(jnp.bfloat16)
    whiten_chunk(x_ref[...], table_ref[...], out_ref)


def whiten_first(x, parts):
    blocks, channels, samples = x.shape
    cos, sin = parts
    whole = lambda a: pl.BlockSpec(a.shape, lambda j: (0,) * a.ndim)
    return pl.pallas_call(
        first_kernel,
        grid=(samples // CHUNK,),
        in_specs=[whole(cos), whole(sin), whole(x)],
        out_specs=[
            pl.BlockSpec((samples, 2 * CHUNK), lambda j: (0, j)),
            pl.BlockSpec((blocks, 2 * channels, CHUNK), lambda j: (0, 0, j)),
        ],
        out_shape=[
            jax.ShapeDtypeStruct((samples, 2 * samples), jnp.bfloat16),
            jax.ShapeDtypeStruct((GROUPS * blocks, 2 * channels, samples), jnp.bfloat16),
        ],
        scratch_shapes=[pltpu.VMEM((samples, LANES), jnp.float32)] * 2,
        compiler_params=pltpu.CompilerParams(vmem_limit_bytes=VMEM),
        cost_estimate=pl.CostEstimate(
            flops=blocks * channels * samples, bytes_accessed=1 << 16, transcendentals=0
        ),
        name="table_and_own",
    )(cos, sin, x)


def next_kernel(x_ref, table_ref, window_ref, out_ref):
    del window_ref
    whiten_chunk(x_ref[...], table_ref[...], out_ref)


def whiten_into(window, place, x, table, name):
    blocks, channels, samples = x.shape
    return pl.pallas_call(
        next_kernel,
        grid=(samples // CHUNK,),
        in_specs=[
            pl.BlockSpec(x.shape, lambda j: (0, 0, 0)),
            pl.BlockSpec((samples, 2 * CHUNK), lambda j: (0, j)),
            pl.BlockSpec(memory_space=pl.ANY),
        ],
        out_specs=pl.BlockSpec((blocks, 2 * channels, CHUNK), lambda j: (place, 0, j)),
        out_shape=jax.ShapeDtypeStruct(window.shape, window.dtype),
        input_output_aliases={2: 0},
        compiler_params=pltpu.CompilerParams(vmem_limit_bytes=VMEM),
        cost_estimate=pl.CostEstimate(
            flops=blocks * channels * samples, bytes_accessed=1 << 16, transcendentals=0
        ),
        name=name,
    )(x, table, window)


def pair_kernel(owner_ref, slots_ref, a0_ref, b0_ref, a1_ref, b1_ref, out_ref):
    del owner_ref
    step = pl.program_id(0)
    channels = a0_ref.shape[1] // 2
    found = []
    for a_ref, b_ref, slot in ((a0_ref, b0_ref, 2 * step), (a1_ref, b1_ref, 2 * step + 1)):
        product = lax.dot_general(
            a_ref[0], b_ref[0], (((1,), (1,)), ((), ())), preferred_element_type=jnp.float32
        )
        real = product[:channels, :channels] + product[channels:, channels:]
        imag = product[channels:, :channels] - product[:channels, channels:]
        live = jnp.where(slots_ref[0, slot] >= 0, 0.25, 0.0)
        both = jnp.concatenate([real, imag], axis=1) * live
        found.append(both.reshape(channels // 8, 8, 2 * channels))
    first, second = found
    row = lax.broadcasted_iota(jnp.int32, first.shape, 1)
    out_ref[:, 0] = jnp.where(row < 4, first, pltpu.roll(second, 4, 1))
    out_ref[:, 1] = jnp.where(row < 4, pltpu.roll(first, 4, 1), second)


def pair_products(window, slots, owner, own_blocks):
    _, stacked, samples = window.shape
    channels = stacked // 2
    slot_count = slots.shape[0]

    def place(owner_ref, slots_ref, which, slot):
        owner = owner_ref[0]
        block = slots_ref[which, slot]
        block = jnp.where(block >= 0, block, owner * own_blocks)
        side = 1 - 2 * lax.rem(owner, 2)
        away = (lax.div(block, own_blocks) - owner) * side
        return lax.rem(away + GROUPS, GROUPS) * own_blocks + lax.rem(block, own_blocks)

    def spec(which, of_two):
        return pl.BlockSpec(
            (1, stacked, samples),
            lambda i, owner_ref, slots_ref: (place(owner_ref, slots_ref, which, 2 * i + of_two), 0, 0),
        )

    return pl.pallas_call(
        pair_kernel,
        grid_spec=pltpu.PrefetchScalarGridSpec(
            num_scalar_prefetch=2,
            grid=(slot_count // 2,),
            in_specs=[spec(0, 0), spec(1, 0), spec(0, 1), spec(1, 1)],
            out_specs=pl.BlockSpec((channels // 8, 2, 8, 2 * channels), lambda i, *_: (0, 0, i, 0)),
        ),
        out_shape=jax.ShapeDtypeStruct((channels // 8, 2, slot_count * 4, 2 * channels), jnp.float32),
        compiler_params=pltpu.CompilerParams(vmem_limit_bytes=VMEM),
        cost_estimate=pl.CostEstimate(
            flops=slot_count * channels * samples, bytes_accessed=1 << 16, transcendentals=0
        ),
        name="pair_products",
    )(owner, slots.T, window, window, window, window)


def on_device(strain, pair_slots):
    x = strain[0]
    blocks, channels, samples = x.shape
    owners = lax.axis_size("chan")
    windows = lax.axis_size("tm")
    slot_count = pair_slots.shape[0]
    owner = lax.axis_index("chan")
    even = range(0, owners, 2)
    odd = range(1, owners, 2)
    sibling_pairs = [(i, i ^ 1) for i in range(owners)]
    near_pairs = [((i + 2) % owners, i) for i in even] + [((i - 2) % owners, i) for i in odd]
    far_pairs = [((i - 2) % owners, i) for i in even] + [((i + 2) % owners, i) for i in odd]

    near = lax.ppermute(x, "chan", near_pairs)
    sibling = lax.ppermute(x, "chan", sibling_pairs)
    table, window = whiten_first(x, table_parts(samples))
    x, window, table = lax.optimization_barrier((x, window, table))
    far = lax.ppermute(x, "chan", far_pairs)
    window = whiten_into(window, 1, sibling, table, "sibling")
    near, window = lax.optimization_barrier((near, window))
    passed = lax.ppermute(near, "chan", sibling_pairs)
    window = whiten_into(window, 2, near, table, "near")
    passed, window = lax.optimization_barrier((passed, window))
    window = whiten_into(window, 4, passed, table, "passed")
    far, window = lax.optimization_barrier((far, window))
    window = whiten_into(window, 3, far, table, "far")

    products = pair_products(window, pair_slots, owner.reshape(1), blocks)
    rows = channels // windows
    products = products.reshape(windows, slot_count * rows, 2 * channels).astype(jnp.float16)
    arrived = lax.all_to_all(products, "tm", 0, 0, tiled=True)
    total = jnp.sum(arrived.astype(jnp.float32), axis=0) * (4.0 / (samples * windows))
    return jnp.transpose(total.reshape(slot_count, rows, 2 * channels), (1, 0, 2))


def solution(mesh):
    return jax.shard_map(
        on_device,
        mesh=mesh,
        in_specs=(P("tm", "chan", None, None), P("chan", None)),
        out_specs=P("tm", "chan", None),
        check_vma=False,
    )
```

```python
import math

import jax
import jax.numpy as jnp
from jax import lax
from jax.experimental import pallas as pl
from jax.experimental.pallas import tpu as pltpu
from jax.sharding import PartitionSpec as P

LANES = 128
CHUNK = 256
ROWS_PERIOD = 16
SPLIT = 32
GROUPS = 5
VMEM = 28 * 1024 * 1024


def table_parts(samples):
    shape = (4 * SPLIT + samples // LANES * ROWS_PERIOD, LANES)
    row = lax.broadcasted_iota(jnp.int32, shape, 0)
    bin_low = lax.broadcasted_iota(jnp.int32, shape, 1) + 1
    part = row // SPLIT
    at = row % SPLIT
    step_row = row - 4 * SPLIT
    phases = jnp.where(
        part == 0,
        bin_low * at * SPLIT,
        jnp.where(
            part == 1,
            bin_low * at,
            jnp.where(
                part == 2,
                2 * SPLIT * at,
                jnp.where(part == 3, 2 * at, (step_row // ROWS_PERIOD) * (step_row % ROWS_PERIOD) * LANES),
            ),
        ),
    )
    angles = (phases % (2 * samples)).astype(jnp.float32) * (math.pi / samples)
    return jnp.cos(angles), jnp.sin(angles)


def whiten_chunk(x, table, out_ref):
    blocks, channels, samples = x.shape
    spectra = jnp.dot(x.reshape(blocks * channels, samples), table, preferred_element_type=jnp.float32)
    for block in range(blocks):
        part = spectra[block * channels : (block + 1) * channels]
        real, imag = part[:, :CHUNK], part[:, CHUNK:]
        power = jnp.sum(real * real + imag * imag, axis=0, keepdims=True) * (1.0 / channels)
        scale = 1.0 / jnp.sqrt(power + 1e-05)
        out_ref[block, :channels, :] = (real * scale).astype(jnp.bfloat16)
        out_ref[block, channels:, :] = (imag * scale).astype(jnp.bfloat16)


def first_kernel(cos_ref, sin_ref, x_ref, table_ref, out_ref, again_ref, low_cos_ref, low_sin_ref):
    chunk = pl.program_id(0)
    samples = x_ref.shape[2]

    @pl.when(chunk == 0)
    def _():
        again_ref[...] = x_ref[...]
        rows = lambda ref, part: ref[part * SPLIT : (part + 1) * SPLIT, :]
        for at in range(samples // SPLIT):
            high = lambda ref, part: ref[part * SPLIT + at : part * SPLIT + at + 1, :]
            taper = 0.5 - 0.5 * (
                high(cos_ref, 2) * rows(cos_ref, 3) - high(sin_ref, 2) * rows(sin_ref, 3)
            )
            cos = high(cos_ref, 0) * rows(cos_ref, 1) - high(sin_ref, 0) * rows(sin_ref, 1)
            sin = high(sin_ref, 0) * rows(cos_ref, 1) + high(cos_ref, 0) * rows(sin_ref, 1)
            low_cos_ref[at * SPLIT : (at + 1) * SPLIT, :] = taper * cos
            low_sin_ref[at * SPLIT : (at + 1) * SPLIT, :] = taper * sin

    shape = (samples // ROWS_PERIOD, ROWS_PERIOD, LANES)
    low_cos = low_cos_ref[...].reshape(shape)
    low_sin = low_sin_ref[...].reshape(shape)
    per_chunk = CHUNK // LANES
    for part in range(per_chunk):
        first_row = 4 * SPLIT + (chunk * per_chunk + part) * ROWS_PERIOD
        step_rows = pl.ds(pl.multiple_of(first_row, ROWS_PERIOD), ROWS_PERIOD)
        step_cos = cos_ref[step_rows, :][None]
        step_sin = sin_ref[step_rows, :][None]
        real = low_cos * step_cos - low_sin * step_sin
        imag = -(low_sin * step_cos + low_cos * step_sin)
        columns = slice(part * LANES, (part + 1) * LANES)
        table_ref[:, columns] = real.reshape(samples, LANES).astype(jnp.bfloat16)
        columns = slice(CHUNK + part * LANES, CHUNK + (part + 1) * LANES)
        table_ref[:, columns] = imag.reshape(samples, LANES).astype(jnp.bfloat16)
    whiten_chunk(x_ref[...], table_ref[...], out_ref)


def hint(work):
    return pl.CostEstimate(flops=work, bytes_accessed=1 << 16, transcendentals=0)


def whiten_first(x, parts):
    blocks, channels, samples = x.shape
    cos, sin = parts
    whole = lambda a: pl.BlockSpec(a.shape, lambda j: (0,) * a.ndim)
    return pl.pallas_call(
        first_kernel,
        grid=(samples // CHUNK,),
        in_specs=[whole(cos), whole(sin), whole(x)],
        out_specs=[
            pl.BlockSpec((samples, 2 * CHUNK), lambda j: (0, j)),
            pl.BlockSpec((blocks, 2 * channels, CHUNK), lambda j: (0, 0, j)),
            whole(x),
        ],
        out_shape=[
            jax.ShapeDtypeStruct((samples, 2 * samples), jnp.bfloat16),
            jax.ShapeDtypeStruct((blocks, 2 * channels, samples), jnp.bfloat16),
            jax.ShapeDtypeStruct(x.shape, x.dtype),
        ],
        scratch_shapes=[pltpu.VMEM((samples, LANES), jnp.float32)] * 2,
        compiler_params=pltpu.CompilerParams(vmem_limit_bytes=VMEM),
        cost_estimate=hint(blocks * channels * samples),
        name="table_and_own",
    )(cos, sin, x)


def next_kernel(x_ref, table_ref, out_ref):
    whiten_chunk(x_ref[...], table_ref[...], out_ref)


def whiten_next(x, table, name):
    blocks, channels, samples = x.shape
    return pl.pallas_call(
        next_kernel,
        grid=(samples // CHUNK,),
        in_specs=[
            pl.BlockSpec(x.shape, lambda j: (0, 0, 0)),
            pl.BlockSpec((samples, 2 * CHUNK), lambda j: (0, j)),
        ],
        out_specs=pl.BlockSpec((blocks, 2 * channels, CHUNK), lambda j: (0, 0, j)),
        out_shape=jax.ShapeDtypeStruct((blocks, 2 * channels, samples), jnp.bfloat16),
        compiler_params=pltpu.CompilerParams(vmem_limit_bytes=VMEM),
        cost_estimate=hint(blocks * channels * samples),
        name=name,
    )(x, table)


def last_kernel(
    owner_ref, slots_ref, x_ref, table_ref, own_ref, sibling_ref, near_ref, passed_ref, out_ref, window_ref, sems
):
    step = pl.program_id(0)
    blocks, channels, samples = x_ref.shape
    chunks = samples // CHUNK
    parts = ((own_ref, 0), (sibling_ref, 1), (near_ref, 2), (passed_ref, 4))
    copies = [
        pltpu.make_async_copy(ref, window_ref.at[pl.ds(place * blocks, blocks)], sems.at[at])
        for at, (ref, place) in enumerate(parts)
    ]

    @pl.when(step == 0)
    def _():
        for copy in copies:
            copy.start()

    for chunk in range(chunks):

        @pl.when(step == chunk)
        def _():
            columns = pl.ds(chunk * CHUNK, CHUNK)
            far = window_ref.at[pl.ds(3 * blocks, blocks), :, columns]
            whiten_chunk(x_ref[...], table_ref[...], far)

    @pl.when(step == chunks - 1)
    def _():
        for copy in copies:
            copy.wait()

    @pl.when(step >= chunks)
    def _():
        owner = owner_ref[0]

        def place(block):
            block = jnp.where(block >= 0, block, owner * blocks)
            away = (lax.div(block, blocks) - owner) * (1 - 2 * lax.rem(owner, 2))
            return lax.rem(away + GROUPS, GROUPS) * blocks + lax.rem(block, blocks)

        found = []
        for slot in (2 * (step - chunks), 2 * (step - chunks) + 1):
            first, second = slots_ref[0, slot], slots_ref[1, slot]
            product = lax.dot_general(
                window_ref[place(first)],
                window_ref[place(second)],
                (((1,), (1,)), ((), ())),
                preferred_element_type=jnp.float32,
            )
            real = product[:channels, :channels] + product[channels:, channels:]
            imag = product[channels:, :channels] - product[:channels, channels:]
            live = jnp.where(first >= 0, 0.25, 0.0)
            both = jnp.concatenate([real, imag], axis=1) * live
            found.append(both.reshape(channels // 8, 8, 2 * channels))
        first, second = found
        row = lax.broadcasted_iota(jnp.int32, first.shape, 1)
        out_ref[:, 0] = jnp.where(row < 4, first, pltpu.roll(second, 4, 1))
        out_ref[:, 1] = jnp.where(row < 4, pltpu.roll(first, 4, 1), second)


def far_and_pairs(owner, slots, x, table, own, sibling, near, passed):
    blocks, channels, samples = x.shape
    slot_count = slots.shape[0]
    chunks = samples // CHUNK
    anywhere = pl.BlockSpec(memory_space=pl.ANY)
    return pl.pallas_call(
        last_kernel,
        grid_spec=pltpu.PrefetchScalarGridSpec(
            num_scalar_prefetch=2,
            grid=(chunks + slot_count // 2,),
            in_specs=[
                pl.BlockSpec(x.shape, lambda i, *_: (0, 0, 0)),
                pl.BlockSpec((samples, 2 * CHUNK), lambda i, *_: (0, jnp.minimum(i, chunks - 1))),
                anywhere,
                anywhere,
                anywhere,
                anywhere,
            ],
            out_specs=pl.BlockSpec(
                (channels // 8, 2, 8, 2 * channels), lambda i, *_: (0, 0, jnp.maximum(i - chunks, 0), 0)
            ),
            scratch_shapes=[
                pltpu.VMEM((GROUPS * blocks, 2 * channels, samples), jnp.bfloat16),
                pltpu.SemaphoreType.DMA((4,)),
            ],
        ),
        out_shape=jax.ShapeDtypeStruct((channels // 8, 2, slot_count * 4, 2 * channels), jnp.float32),
        compiler_params=pltpu.CompilerParams(vmem_limit_bytes=VMEM),
        cost_estimate=hint(slot_count * channels * samples),
        name="far_and_pairs",
    )(owner, slots.T, x, table, own, sibling, near, passed)


def after_transfer(x, work):
    anywhere = pl.BlockSpec(memory_space=pl.ANY)
    return pl.pallas_call(
        lambda x_ref, out_ref: None,
        in_specs=[anywhere],
        out_specs=anywhere,
        out_shape=jax.ShapeDtypeStruct(x.shape, x.dtype),
        input_output_aliases={0: 0},
        cost_estimate=hint(work),
        name="far_arrived",
    )(x)


def on_device(strain, pair_slots):
    x = strain[0]
    blocks, channels, samples = x.shape
    owners = lax.axis_size("chan")
    windows = lax.axis_size("tm")
    slot_count = pair_slots.shape[0]
    owner = lax.axis_index("chan")
    even = range(0, owners, 2)
    odd = range(1, owners, 2)
    sibling_pairs = [(i, i ^ 1) for i in range(owners)]
    near_pairs = [((i + 2) % owners, i) for i in even] + [((i - 2) % owners, i) for i in odd]
    far_pairs = [((i - 2) % owners, i) for i in even] + [((i + 2) % owners, i) for i in odd]

    near = lax.ppermute(x, "chan", near_pairs)
    table, own, again = whiten_first(x, table_parts(samples))
    sibling = lax.ppermute(own, "chan", sibling_pairs)
    far = lax.ppermute(again, "chan", far_pairs)
    far = after_transfer(far, 100 * 10**9)
    near = whiten_next(near, table, "near")
    passed = lax.ppermute(near, "chan", sibling_pairs)
    products = far_and_pairs(owner.reshape(1), pair_slots, far, table, own, sibling, near, passed)

    rows = channels // windows
    products = products.reshape(windows, slot_count * rows, 2 * channels).astype(jnp.float16)
    arrived = lax.all_to_all(products, "tm", 0, 0, tiled=True)
    total = jnp.sum(arrived.astype(jnp.float32), axis=0) * (4.0 / (samples * windows))
    return jnp.transpose(total.reshape(slot_count, rows, 2 * channels), (1, 0, 2))


def solution(mesh):
    return jax.shard_map(
        on_device,
        mesh=mesh,
        in_specs=(P("tm", "chan", None, None), P("chan", None)),
        out_specs=P("tm", "chan", None),
        check_vma=False,
    )
```

```python
import math

import jax
import jax.numpy as jnp
from jax import lax
from jax.experimental import pallas as pl
from jax.experimental.pallas import tpu as pltpu
from jax.sharding import PartitionSpec as P

LANES = 128
ROWS_PERIOD = 16
SPLIT = 32
GROUPS = 5
SLOTS_PER_STEP = 6
MIB = 1024 * 1024


def table_parts(samples):
    shape = (4 * SPLIT + samples // LANES * ROWS_PERIOD, LANES)
    row = lax.broadcasted_iota(jnp.int32, shape, 0)
    bin_low = lax.broadcasted_iota(jnp.int32, shape, 1) + 1
    part = row // SPLIT
    at = row % SPLIT
    step_row = row - 4 * SPLIT
    phases = jnp.where(
        part == 0,
        bin_low * at * SPLIT,
        jnp.where(
            part == 1,
            bin_low * at,
            jnp.where(
                part == 2,
                2 * SPLIT * at,
                jnp.where(part == 3, 2 * at, (step_row // ROWS_PERIOD) * (step_row % ROWS_PERIOD) * LANES),
            ),
        ),
    )
    angles = (phases % (2 * samples)).astype(jnp.float32) * (math.pi / samples)
    return jnp.cos(angles), jnp.sin(angles)


def whiten_bins(x, table, out_ref, bins):
    blocks, channels, samples = x.shape
    spectra = jnp.dot(x.reshape(blocks * channels, samples), table, preferred_element_type=jnp.float32)
    for block in range(blocks):
        part = spectra[block * channels : (block + 1) * channels]
        real, imag = part[:, :LANES], part[:, LANES:]
        power = jnp.sum(real * real + imag * imag, axis=0, keepdims=True) * (1.0 / channels)
        scale = 1.0 / jnp.sqrt(power + 1e-05)
        out_ref[block, :channels, bins] = (real * scale).astype(jnp.bfloat16)
        out_ref[block, channels:, bins] = (imag * scale).astype(jnp.bfloat16)


def first_kernel(cos_ref, sin_ref, x_ref, table_ref, out_ref, again_ref, low_cos_ref, low_sin_ref):
    samples = x_ref.shape[2]
    again_ref[...] = x_ref[...]
    rows = lambda ref, part: ref[part * SPLIT : (part + 1) * SPLIT, :]
    for at in range(samples // SPLIT):
        high = lambda ref, part: ref[part * SPLIT + at : part * SPLIT + at + 1, :]
        taper = 0.5 - 0.5 * (high(cos_ref, 2) * rows(cos_ref, 3) - high(sin_ref, 2) * rows(sin_ref, 3))
        cos = high(cos_ref, 0) * rows(cos_ref, 1) - high(sin_ref, 0) * rows(sin_ref, 1)
        sin = high(sin_ref, 0) * rows(cos_ref, 1) + high(cos_ref, 0) * rows(sin_ref, 1)
        low_cos_ref[at * SPLIT : (at + 1) * SPLIT, :] = taper * cos
        low_sin_ref[at * SPLIT : (at + 1) * SPLIT, :] = taper * sin

    shape = (samples // ROWS_PERIOD, ROWS_PERIOD, LANES)
    for step in range(samples // LANES):
        low_cos = low_cos_ref[...].reshape(shape)
        low_sin = low_sin_ref[...].reshape(shape)
        step_rows = slice(4 * SPLIT + step * ROWS_PERIOD, 4 * SPLIT + (step + 1) * ROWS_PERIOD)
        step_cos = cos_ref[step_rows, :][None]
        step_sin = sin_ref[step_rows, :][None]
        real = low_cos * step_cos - low_sin * step_sin
        imag = -(low_sin * step_cos + low_cos * step_sin)
        columns = slice(2 * step * LANES, (2 * step + 1) * LANES)
        table_ref[:, columns] = real.reshape(samples, LANES).astype(jnp.bfloat16)
        columns = slice((2 * step + 1) * LANES, (2 * step + 2) * LANES)
        table_ref[:, columns] = imag.reshape(samples, LANES).astype(jnp.bfloat16)
    whiten_all(x_ref, table_ref, out_ref)


def whiten_all(x_ref, table_ref, out_ref):
    x = x_ref[...]
    for step in range(x.shape[2] // LANES):
        table = table_ref[:, 2 * step * LANES : 2 * (step + 1) * LANES]
        whiten_bins(x, table, out_ref, slice(step * LANES, (step + 1) * LANES))


def hint(work):
    return pl.CostEstimate(flops=work, bytes_accessed=1 << 16, transcendentals=0)


def pinned(*arrays):
    return tuple(pltpu.with_memory_space_constraint(array, pltpu.VMEM) for array in arrays)


HERE = pl.BlockSpec(memory_space=pltpu.VMEM)


def whiten_first(x, parts):
    blocks, channels, samples = x.shape
    return pl.pallas_call(
        first_kernel,
        in_specs=[HERE] * 3,
        out_specs=[HERE] * 3,
        out_shape=[
            pltpu.VMEM((samples, 2 * samples), jnp.bfloat16),
            pltpu.VMEM((blocks, 2 * channels, samples), jnp.bfloat16),
            pltpu.VMEM(x.shape, x.dtype),
        ],
        scratch_shapes=[pltpu.VMEM((samples, LANES), jnp.float32)] * 2,
        compiler_params=pltpu.CompilerParams(vmem_limit_bytes=12 * MIB),
        cost_estimate=hint(blocks * channels * samples),
        name="table_and_own",
    )(*pinned(*parts, x))


def whiten_next(x, table, name):
    blocks, channels, samples = x.shape
    return pl.pallas_call(
        whiten_all,
        in_specs=[HERE] * 2,
        out_specs=HERE,
        out_shape=pltpu.VMEM((blocks, 2 * channels, samples), jnp.bfloat16),
        compiler_params=pltpu.CompilerParams(vmem_limit_bytes=12 * MIB),
        cost_estimate=hint(blocks * channels * samples),
        name=name,
    )(*pinned(x, table))


def last_kernel(
    owner_ref, slots_ref, x_ref, table_ref, own_ref, sibling_ref, near_ref, passed_ref, out_ref, window_ref, sems
):
    step = pl.program_id(0)
    blocks, channels, samples = x_ref.shape

    @pl.when(step == 0)
    def _():
        parts = ((own_ref, 0), (sibling_ref, 1), (near_ref, 2), (passed_ref, 4))
        copies = [
            pltpu.make_async_copy(ref, window_ref.at[pl.ds(place * blocks, blocks)], sems.at[at])
            for at, (ref, place) in enumerate(parts)
        ]
        for copy in copies:
            copy.start()
        whiten_all(x_ref, table_ref, window_ref.at[pl.ds(3 * blocks, blocks)])
        for copy in copies:
            copy.wait()

    @pl.when(step > 0)
    def _():
        owner = owner_ref[0]

        def place(block):
            block = jnp.where(block >= 0, block, owner * blocks)
            away = (lax.div(block, blocks) - owner) * (1 - 2 * lax.rem(owner, 2))
            return lax.rem(away + GROUPS, GROUPS) * blocks + lax.rem(block, blocks)

        found = []
        for at in range(SLOTS_PER_STEP):
            slot = (step - 1) * SLOTS_PER_STEP + at
            first, second = slots_ref[0, slot], slots_ref[1, slot]
            product = lax.dot_general(
                window_ref[place(first)],
                window_ref[place(second)],
                (((1,), (1,)), ((), ())),
                preferred_element_type=jnp.float32,
            )
            real = product[:channels, :channels] + product[channels:, channels:]
            imag = product[channels:, :channels] - product[:channels, channels:]
            live = jnp.where(first >= 0, 0.25, 0.0)
            both = jnp.concatenate([real, imag], axis=1) * live
            found.append(both.reshape(channels // 8, 8, 2 * channels))
        for pair in range(SLOTS_PER_STEP // 2):
            first, second = found[2 * pair], found[2 * pair + 1]
            row = lax.broadcasted_iota(jnp.int32, first.shape, 1)
            rows = slice(8 * pair, 8 * (pair + 1))
            out_ref[:, 0, rows] = jnp.where(row < 4, first, pltpu.roll(second, 4, 1))
            out_ref[:, 1, rows] = jnp.where(row < 4, pltpu.roll(first, 4, 1), second)


def far_and_pairs(owner, slots, x, table, own, sibling, near, passed):
    blocks, channels, samples = x.shape
    slot_count = slots.shape[0]
    return pl.pallas_call(
        last_kernel,
        grid_spec=pltpu.PrefetchScalarGridSpec(
            num_scalar_prefetch=2,
            grid=(1 + slot_count // SLOTS_PER_STEP,),
            in_specs=[HERE] * 6,
            out_specs=pl.BlockSpec(
                (channels // 8, 2, 4 * SLOTS_PER_STEP, 2 * channels), lambda i, *_: (0, 0, jnp.maximum(i - 1, 0), 0)
            ),
            scratch_shapes=[
                pltpu.VMEM((GROUPS * blocks, 2 * channels, samples), jnp.bfloat16),
                pltpu.SemaphoreType.DMA((4,)),
            ],
        ),
        out_shape=pltpu.VMEM((channels // 8, 2, slot_count * 4, 2 * channels), jnp.float32),
        compiler_params=pltpu.CompilerParams(vmem_limit_bytes=20 * MIB),
        cost_estimate=hint(slot_count * channels * samples),
        name="far_and_pairs",
    )(owner, slots.T, *pinned(x, table, own, sibling, near, passed))


def after_transfer(x, work):
    anywhere = pl.BlockSpec(memory_space=pl.ANY)
    return pl.pallas_call(
        lambda x_ref, out_ref: None,
        in_specs=[anywhere],
        out_specs=anywhere,
        out_shape=jax.ShapeDtypeStruct(x.shape, x.dtype),
        input_output_aliases={0: 0},
        cost_estimate=hint(work),
        name="far_arrived",
    )(x)


def on_device(strain, pair_slots):
    x = strain[0]
    blocks, channels, samples = x.shape
    owners = lax.axis_size("chan")
    windows = lax.axis_size("tm")
    slot_count = pair_slots.shape[0]
    owner = lax.axis_index("chan")
    even = range(0, owners, 2)
    odd = range(1, owners, 2)
    sibling_pairs = [(i, i ^ 1) for i in range(owners)]
    near_pairs = [((i + 2) % owners, i) for i in even] + [((i - 2) % owners, i) for i in odd]
    far_pairs = [((i - 2) % owners, i) for i in even] + [((i + 2) % owners, i) for i in odd]

    near = lax.ppermute(x, "chan", near_pairs)
    table, own, again = whiten_first(x, table_parts(samples))
    sibling = lax.ppermute(own, "chan", sibling_pairs)
    far = lax.ppermute(again, "chan", far_pairs)
    far = after_transfer(far, 100 * 10**9)
    near = whiten_next(near, table, "near")
    passed = lax.ppermute(near, "chan", sibling_pairs)
    products = far_and_pairs(owner.reshape(1), pair_slots, far, table, own, sibling, near, passed)

    rows = channels // windows
    products = products.reshape(windows, slot_count * rows, 2 * channels).astype(jnp.float16)
    arrived = lax.all_to_all(products, "tm", 0, 0, tiled=True)
    total = jnp.sum(arrived.astype(jnp.float32), axis=0) * (4.0 / (samples * windows))
    return jnp.transpose(total.reshape(slot_count, rows, 2 * channels), (1, 0, 2))


def solution(mesh):
    return jax.shard_map(
        on_device,
        mesh=mesh,
        in_specs=(P("tm", "chan", None, None), P("chan", None)),
        out_specs=P("tm", "chan", None),
        check_vma=False,
    )
```

```python
import math

import jax
import jax.numpy as jnp
from jax import lax
from jax.experimental import pallas as pl
from jax.experimental.pallas import tpu as pltpu
from jax.sharding import PartitionSpec as P

LANES = 128
ROWS_PERIOD = 16
SPLIT = 32
GROUPS = 5
SLOTS_PER_STEP = 6
MIB = 1024 * 1024


def table_parts(samples):
    shape = (4 * SPLIT + samples // LANES * ROWS_PERIOD, LANES)
    row = lax.broadcasted_iota(jnp.int32, shape, 0)
    bin_low = lax.broadcasted_iota(jnp.int32, shape, 1) + 1
    part = row // SPLIT
    at = row % SPLIT
    step_row = row - 4 * SPLIT
    phases = jnp.where(
        part == 0,
        bin_low * at * SPLIT,
        jnp.where(
            part == 1,
            bin_low * at,
            jnp.where(
                part == 2,
                2 * SPLIT * at,
                jnp.where(part == 3, 2 * at, (step_row // ROWS_PERIOD) * (step_row % ROWS_PERIOD) * LANES),
            ),
        ),
    )
    angles = (phases % (2 * samples)).astype(jnp.float32) * (math.pi / samples)
    return jnp.cos(angles), jnp.sin(angles)


def whiten_bins(x, table, out_ref, bins):
    blocks, channels, samples = x.shape
    spectra = jnp.dot(x.reshape(blocks * channels, samples), table, preferred_element_type=jnp.float32)
    for block in range(blocks):
        part = spectra[block * channels : (block + 1) * channels]
        real, imag = part[:, :LANES], part[:, LANES:]
        power = jnp.sum(real * real + imag * imag, axis=0, keepdims=True) * (1.0 / channels)
        scale = 1.0 / jnp.sqrt(power + 1e-05)
        out_ref[block, :channels, bins] = (real * scale).astype(jnp.bfloat16)
        out_ref[block, channels:, bins] = (imag * scale).astype(jnp.bfloat16)


def first_kernel(cos_ref, sin_ref, x_ref, table_ref, out_ref, again_ref, low_cos_ref, low_sin_ref, sem):
    samples = x_ref.shape[2]
    fetch = pltpu.make_async_copy(x_ref, again_ref, sem)
    fetch.start()
    rows = lambda ref, part: ref[part * SPLIT : (part + 1) * SPLIT, :]
    for at in range(samples // SPLIT):
        high = lambda ref, part: ref[part * SPLIT + at : part * SPLIT + at + 1, :]
        taper = 0.5 - 0.5 * (high(cos_ref, 2) * rows(cos_ref, 3) - high(sin_ref, 2) * rows(sin_ref, 3))
        cos = high(cos_ref, 0) * rows(cos_ref, 1) - high(sin_ref, 0) * rows(sin_ref, 1)
        sin = high(sin_ref, 0) * rows(cos_ref, 1) + high(cos_ref, 0) * rows(sin_ref, 1)
        low_cos_ref[at * SPLIT : (at + 1) * SPLIT, :] = taper * cos
        low_sin_ref[at * SPLIT : (at + 1) * SPLIT, :] = taper * sin

    shape = (samples // ROWS_PERIOD, ROWS_PERIOD, LANES)
    for step in range(samples // LANES):
        low_cos = low_cos_ref[...].reshape(shape)
        low_sin = low_sin_ref[...].reshape(shape)
        step_rows = slice(4 * SPLIT + step * ROWS_PERIOD, 4 * SPLIT + (step + 1) * ROWS_PERIOD)
        step_cos = cos_ref[step_rows, :][None]
        step_sin = sin_ref[step_rows, :][None]
        real = low_cos * step_cos - low_sin * step_sin
        imag = -(low_sin * step_cos + low_cos * step_sin)
        columns = slice(2 * step * LANES, (2 * step + 1) * LANES)
        table_ref[:, columns] = real.reshape(samples, LANES).astype(jnp.bfloat16)
        columns = slice((2 * step + 1) * LANES, (2 * step + 2) * LANES)
        table_ref[:, columns] = imag.reshape(samples, LANES).astype(jnp.bfloat16)
    fetch.wait()
    whiten_all(again_ref, table_ref, out_ref)


def whiten_all(x_ref, table_ref, out_ref):
    x = x_ref[...]
    for step in range(x.shape[2] // LANES):
        table = table_ref[:, 2 * step * LANES : 2 * (step + 1) * LANES]
        whiten_bins(x, table, out_ref, slice(step * LANES, (step + 1) * LANES))


def hint(work):
    return pl.CostEstimate(flops=work, bytes_accessed=1 << 16, transcendentals=0)


def pinned(*arrays):
    return tuple(pltpu.with_memory_space_constraint(array, pltpu.VMEM) for array in arrays)


HERE = pl.BlockSpec(memory_space=pltpu.VMEM)


def whiten_first(x, parts):
    blocks, channels, samples = x.shape
    return pl.pallas_call(
        first_kernel,
        in_specs=[HERE, HERE, pl.BlockSpec(memory_space=pl.ANY)],
        out_specs=[HERE] * 3,
        out_shape=[
            pltpu.VMEM((samples, 2 * samples), jnp.bfloat16),
            pltpu.VMEM((blocks, 2 * channels, samples), jnp.bfloat16),
            pltpu.VMEM(x.shape, x.dtype),
        ],
        scratch_shapes=[pltpu.VMEM((samples, LANES), jnp.float32)] * 2 + [pltpu.SemaphoreType.DMA],
        compiler_params=pltpu.CompilerParams(vmem_limit_bytes=12 * MIB),
        cost_estimate=hint(blocks * channels * samples),
        name="table_and_own",
    )(*pinned(*parts), pltpu.with_memory_space_constraint(x, pltpu.HBM))


def whiten_next(x, table, name):
    blocks, channels, samples = x.shape
    return pl.pallas_call(
        whiten_all,
        in_specs=[HERE] * 2,
        out_specs=HERE,
        out_shape=pltpu.VMEM((blocks, 2 * channels, samples), jnp.bfloat16),
        compiler_params=pltpu.CompilerParams(vmem_limit_bytes=12 * MIB),
        cost_estimate=hint(blocks * channels * samples),
        name=name,
    )(*pinned(x, table))


def last_kernel(
    owner_ref, slots_ref, x_ref, table_ref, own_ref, sibling_ref, near_ref, passed_ref, out_ref, window_ref, sems
):
    step = pl.program_id(0)
    blocks, channels, samples = x_ref.shape

    @pl.when(step == 0)
    def _():
        parts = ((own_ref, 0), (sibling_ref, 1), (near_ref, 2), (passed_ref, 4))
        copies = [
            pltpu.make_async_copy(ref, window_ref.at[pl.ds(place * blocks, blocks)], sems.at[at])
            for at, (ref, place) in enumerate(parts)
        ]
        for copy in copies:
            copy.start()
        whiten_all(x_ref, table_ref, window_ref.at[pl.ds(3 * blocks, blocks)])
        for copy in copies:
            copy.wait()

    @pl.when(step > 0)
    def _():
        owner = owner_ref[0]

        def place(block):
            block = jnp.where(block >= 0, block, owner * blocks)
            away = (lax.div(block, blocks) - owner) * (1 - 2 * lax.rem(owner, 2))
            return lax.rem(away + GROUPS, GROUPS) * blocks + lax.rem(block, blocks)

        found = []
        for at in range(SLOTS_PER_STEP):
            slot = (step - 1) * SLOTS_PER_STEP + at
            first, second = slots_ref[0, slot], slots_ref[1, slot]
            product = lax.dot_general(
                window_ref[place(first)],
                window_ref[place(second)],
                (((1,), (1,)), ((), ())),
                preferred_element_type=jnp.float32,
            )
            real = product[:channels, :channels] + product[channels:, channels:]
            imag = product[channels:, :channels] - product[:channels, channels:]
            live = jnp.where(first >= 0, 0.25, 0.0)
            both = jnp.concatenate([real, imag], axis=1) * live
            found.append(both.reshape(channels // 8, 8, 2 * channels))
        for pair in range(SLOTS_PER_STEP // 2):
            first, second = found[2 * pair], found[2 * pair + 1]
            row = lax.broadcasted_iota(jnp.int32, first.shape, 1)
            rows = slice(8 * pair, 8 * (pair + 1))
            out_ref[:, 0, rows] = jnp.where(row < 4, first, pltpu.roll(second, 4, 1))
            out_ref[:, 1, rows] = jnp.where(row < 4, pltpu.roll(first, 4, 1), second)


def far_and_pairs(owner, slots, x, table, own, sibling, near, passed):
    blocks, channels, samples = x.shape
    slot_count = slots.shape[0]
    return pl.pallas_call(
        last_kernel,
        grid_spec=pltpu.PrefetchScalarGridSpec(
            num_scalar_prefetch=2,
            grid=(1 + slot_count // SLOTS_PER_STEP,),
            in_specs=[HERE] * 6,
            out_specs=pl.BlockSpec(
                (channels // 8, 2, 4 * SLOTS_PER_STEP, 2 * channels), lambda i, *_: (0, 0, jnp.maximum(i - 1, 0), 0)
            ),
            scratch_shapes=[
                pltpu.VMEM((GROUPS * blocks, 2 * channels, samples), jnp.bfloat16),
                pltpu.SemaphoreType.DMA((4,)),
            ],
        ),
        out_shape=pltpu.VMEM((channels // 8, 2, slot_count * 4, 2 * channels), jnp.float32),
        compiler_params=pltpu.CompilerParams(vmem_limit_bytes=20 * MIB),
        cost_estimate=hint(slot_count * channels * samples),
        name="far_and_pairs",
    )(owner, slots.T, *pinned(x, table, own, sibling, near, passed))


def after_transfer(x, work):
    anywhere = pl.BlockSpec(memory_space=pl.ANY)
    return pl.pallas_call(
        lambda x_ref, out_ref: None,
        in_specs=[anywhere],
        out_specs=anywhere,
        out_shape=jax.ShapeDtypeStruct(x.shape, x.dtype),
        input_output_aliases={0: 0},
        compiler_params=pltpu.CompilerParams(vmem_limit_bytes=MIB),
        cost_estimate=hint(work),
        name="far_arrived",
    )(x)


def on_device(strain, pair_slots):
    x = strain[0]
    blocks, channels, samples = x.shape
    owners = lax.axis_size("chan")
    windows = lax.axis_size("tm")
    slot_count = pair_slots.shape[0]
    owner = lax.axis_index("chan")
    even = range(0, owners, 2)
    odd = range(1, owners, 2)
    sibling_pairs = [(i, i ^ 1) for i in range(owners)]
    near_pairs = [((i + 2) % owners, i) for i in even] + [((i - 2) % owners, i) for i in odd]
    far_pairs = [((i - 2) % owners, i) for i in even] + [((i + 2) % owners, i) for i in odd]

    near = lax.ppermute(x, "chan", near_pairs)
    table, own, again = whiten_first(x, table_parts(samples))
    sibling = lax.ppermute(own, "chan", sibling_pairs)
    far = lax.ppermute(again, "chan", far_pairs)
    far = after_transfer(far, 100 * 10**9)
    near = whiten_next(near, table, "near")
    passed = lax.ppermute(near, "chan", sibling_pairs)
    products = far_and_pairs(owner.reshape(1), pair_slots, far, table, own, sibling, near, passed)

    rows = channels // windows
    products = products.reshape(windows, slot_count * rows, 2 * channels).astype(jnp.float16)
    arrived = lax.all_to_all(products, "tm", 0, 0, tiled=True)
    total = jnp.sum(arrived.astype(jnp.float32), axis=0) * (4.0 / (samples * windows))
    return jnp.transpose(total.reshape(slot_count, rows, 2 * channels), (1, 0, 2))


def solution(mesh):
    return jax.shard_map(
        on_device,
        mesh=mesh,
        in_specs=(P("tm", "chan", None, None), P("chan", None)),
        out_specs=P("tm", "chan", None),
        check_vma=False,
    )
```

```python
import math

import jax
import jax.numpy as jnp
from jax import lax
from jax.experimental import pallas as pl
from jax.experimental.pallas import tpu as pltpu
from jax.sharding import PartitionSpec as P

LANES = 128
ROWS_PERIOD = 16
SPLIT = 32
GROUPS = 5
SLOTS_PER_STEP = 6
MIB = 1024 * 1024


def table_parts(samples):
    shape = (4 * SPLIT + samples // LANES * ROWS_PERIOD, LANES)
    row = lax.broadcasted_iota(jnp.int32, shape, 0)
    bin_low = lax.broadcasted_iota(jnp.int32, shape, 1) + 1
    part = row // SPLIT
    at = row % SPLIT
    step_row = row - 4 * SPLIT
    phases = jnp.where(
        part == 0,
        bin_low * at * SPLIT,
        jnp.where(
            part == 1,
            bin_low * at,
            jnp.where(
                part == 2,
                2 * SPLIT * at,
                jnp.where(part == 3, 2 * at, (step_row // ROWS_PERIOD) * (step_row % ROWS_PERIOD) * LANES),
            ),
        ),
    )
    angles = (phases % (2 * samples)).astype(jnp.float32) * (math.pi / samples)
    return jnp.cos(angles), jnp.sin(angles)


def whiten_bins(x, table, out_ref, bins):
    blocks, channels, samples = x.shape
    spectra = jnp.dot(x.reshape(blocks * channels, samples), table, preferred_element_type=jnp.float32)
    for block in range(blocks):
        part = spectra[block * channels : (block + 1) * channels]
        real, imag = part[:, :LANES], part[:, LANES:]
        power = jnp.sum(real * real + imag * imag, axis=0, keepdims=True) * (1.0 / channels)
        scale = 1.0 / jnp.sqrt(power + 1e-05)
        out_ref[block, :channels, bins] = (real * scale).astype(jnp.bfloat16)
        out_ref[block, channels:, bins] = (imag * scale).astype(jnp.bfloat16)


def first_kernel(cos_ref, sin_ref, x_ref, table_ref, out_ref, again_ref, low_cos_ref, low_sin_ref, sem):
    samples = x_ref.shape[2]
    fetch = pltpu.make_async_copy(x_ref, again_ref, sem)
    fetch.start()
    rows = lambda ref, part: ref[part * SPLIT : (part + 1) * SPLIT, :]
    for at in range(samples // SPLIT):
        high = lambda ref, part: ref[part * SPLIT + at : part * SPLIT + at + 1, :]
        taper = 0.5 - 0.5 * (high(cos_ref, 2) * rows(cos_ref, 3) - high(sin_ref, 2) * rows(sin_ref, 3))
        cos = high(cos_ref, 0) * rows(cos_ref, 1) - high(sin_ref, 0) * rows(sin_ref, 1)
        sin = high(sin_ref, 0) * rows(cos_ref, 1) + high(cos_ref, 0) * rows(sin_ref, 1)
        low_cos_ref[at * SPLIT : (at + 1) * SPLIT, :] = taper * cos
        low_sin_ref[at * SPLIT : (at + 1) * SPLIT, :] = taper * sin

    shape = (samples // ROWS_PERIOD, ROWS_PERIOD, LANES)
    for step in range(samples // LANES):
        low_cos = low_cos_ref[...].reshape(shape)
        low_sin = low_sin_ref[...].reshape(shape)
        step_rows = slice(4 * SPLIT + step * ROWS_PERIOD, 4 * SPLIT + (step + 1) * ROWS_PERIOD)
        step_cos = cos_ref[step_rows, :][None]
        step_sin = sin_ref[step_rows, :][None]
        real = low_cos * step_cos - low_sin * step_sin
        imag = -(low_sin * step_cos + low_cos * step_sin)
        columns = slice(2 * step * LANES, (2 * step + 1) * LANES)
        table_ref[:, columns] = real.reshape(samples, LANES).astype(jnp.bfloat16)
        columns = slice((2 * step + 1) * LANES, (2 * step + 2) * LANES)
        table_ref[:, columns] = imag.reshape(samples, LANES).astype(jnp.bfloat16)
    fetch.wait()
    whiten_all(again_ref, table_ref, out_ref)


def whiten_all(x_ref, table_ref, out_ref):
    x = x_ref[...]
    for step in range(x.shape[2] // LANES):
        table = table_ref[:, 2 * step * LANES : 2 * (step + 1) * LANES]
        whiten_bins(x, table, out_ref, slice(step * LANES, (step + 1) * LANES))


def hint(work):
    return pl.CostEstimate(flops=work, bytes_accessed=1 << 16, transcendentals=0)


def pinned(*arrays):
    return tuple(pltpu.with_memory_space_constraint(array, pltpu.VMEM) for array in arrays)


HERE = pl.BlockSpec(memory_space=pltpu.VMEM)


def whiten_first(x, parts):
    blocks, channels, samples = x.shape
    return pl.pallas_call(
        first_kernel,
        in_specs=[HERE, HERE, pl.BlockSpec(memory_space=pl.ANY)],
        out_specs=[HERE] * 3,
        out_shape=[
            pltpu.VMEM((samples, 2 * samples), jnp.bfloat16),
            pltpu.VMEM((blocks, 2 * channels, samples), jnp.bfloat16),
            pltpu.VMEM(x.shape, x.dtype),
        ],
        scratch_shapes=[pltpu.VMEM((samples, LANES), jnp.float32)] * 2 + [pltpu.SemaphoreType.DMA],
        compiler_params=pltpu.CompilerParams(vmem_limit_bytes=12 * MIB),
        cost_estimate=hint(blocks * channels * samples),
        name="table_and_own",
    )(*pinned(*parts), pltpu.with_memory_space_constraint(x, pltpu.HBM))


def whiten_next(x, table, name):
    blocks, channels, samples = x.shape
    return pl.pallas_call(
        whiten_all,
        in_specs=[HERE] * 2,
        out_specs=HERE,
        out_shape=pltpu.VMEM((blocks, 2 * channels, samples), jnp.bfloat16),
        compiler_params=pltpu.CompilerParams(vmem_limit_bytes=12 * MIB),
        cost_estimate=hint(blocks * channels * samples),
        name=name,
    )(*pinned(x, table))


def last_kernel(
    slots_ref, x_ref, table_ref, own_ref, sibling_ref, near_ref, passed_ref, out_ref, window_ref, sems
):
    step = pl.program_id(0)
    blocks, channels, samples = x_ref.shape

    @pl.when(step == 0)
    def _():
        parts = ((own_ref, 0), (sibling_ref, 1), (near_ref, 2), (passed_ref, 4))
        copies = [
            pltpu.make_async_copy(ref, window_ref.at[pl.ds(place * blocks, blocks)], sems.at[at])
            for at, (ref, place) in enumerate(parts)
        ]
        for copy in copies:
            copy.start()
        whiten_all(x_ref, table_ref, window_ref.at[pl.ds(3 * blocks, blocks)])
        for copy in copies:
            copy.wait()

    @pl.when(step > 0)
    def _():
        owner = lax.axis_index("chan")

        def place(block):
            block = jnp.where(block >= 0, block, owner * blocks)
            away = (lax.div(block, blocks) - owner) * (1 - 2 * lax.rem(owner, 2))
            return lax.rem(away + GROUPS, GROUPS) * blocks + lax.rem(block, blocks)

        found = []
        for at in range(SLOTS_PER_STEP):
            slot = (step - 1) * SLOTS_PER_STEP + at
            first, second = slots_ref[0, slot], slots_ref[1, slot]
            product = lax.dot_general(
                window_ref[place(first)],
                window_ref[place(second)],
                (((1,), (1,)), ((), ())),
                preferred_element_type=jnp.float32,
            )
            real = product[:channels, :channels] + product[channels:, channels:]
            imag = product[channels:, :channels] - product[:channels, channels:]
            live = jnp.where(first >= 0, 0.25, 0.0)
            both = jnp.concatenate([real, imag], axis=1) * live
            found.append(both.reshape(channels // 8, 8, 2 * channels))
        for pair in range(SLOTS_PER_STEP // 2):
            first, second = found[2 * pair], found[2 * pair + 1]
            row = lax.broadcasted_iota(jnp.int32, first.shape, 1)
            rows = slice(8 * pair, 8 * (pair + 1))
            out_ref[:, 0, rows] = jnp.where(row < 4, first, pltpu.roll(second, 4, 1))
            out_ref[:, 1, rows] = jnp.where(row < 4, pltpu.roll(first, 4, 1), second)


def far_and_pairs(slots, x, table, own, sibling, near, passed):
    blocks, channels, samples = x.shape
    slot_count = slots.shape[0]
    return pl.pallas_call(
        last_kernel,
        grid_spec=pltpu.PrefetchScalarGridSpec(
            num_scalar_prefetch=1,
            grid=(1 + slot_count // SLOTS_PER_STEP,),
            in_specs=[HERE] * 6,
            out_specs=pl.BlockSpec(
                (channels // 8, 2, 4 * SLOTS_PER_STEP, 2 * channels), lambda i, *_: (0, 0, jnp.maximum(i - 1, 0), 0)
            ),
            scratch_shapes=[
                pltpu.VMEM((GROUPS * blocks, 2 * channels, samples), jnp.bfloat16),
                pltpu.SemaphoreType.DMA((4,)),
            ],
        ),
        out_shape=pltpu.VMEM((channels // 8, 2, slot_count * 4, 2 * channels), jnp.float32),
        compiler_params=pltpu.CompilerParams(vmem_limit_bytes=20 * MIB),
        cost_estimate=hint(slot_count * channels * samples),
        name="far_and_pairs",
    )(slots.T, *pinned(x, table, own, sibling, near, passed))


def after_transfer(x, work):
    anywhere = pl.BlockSpec(memory_space=pl.ANY)
    return pl.pallas_call(
        lambda x_ref, out_ref: None,
        in_specs=[anywhere],
        out_specs=anywhere,
        out_shape=jax.ShapeDtypeStruct(x.shape, x.dtype),
        input_output_aliases={0: 0},
        compiler_params=pltpu.CompilerParams(vmem_limit_bytes=MIB),
        cost_estimate=hint(work),
        name="far_arrived",
    )(x)


def on_device(strain, pair_slots):
    x = strain[0]
    blocks, channels, samples = x.shape
    owners = lax.axis_size("chan")
    windows = lax.axis_size("tm")
    slot_count = pair_slots.shape[0]
    even = range(0, owners, 2)
    odd = range(1, owners, 2)
    sibling_pairs = [(i, i ^ 1) for i in range(owners)]
    near_pairs = [((i + 2) % owners, i) for i in even] + [((i - 2) % owners, i) for i in odd]
    far_pairs = [((i - 2) % owners, i) for i in even] + [((i + 2) % owners, i) for i in odd]

    near = lax.ppermute(x, "chan", near_pairs)
    table, own, again = whiten_first(x, table_parts(samples))
    sibling = lax.ppermute(own, "chan", sibling_pairs)
    far = lax.ppermute(again, "chan", far_pairs)
    far = after_transfer(far, 100 * 10**9)
    near = whiten_next(near, table, "near")
    passed = lax.ppermute(near, "chan", sibling_pairs)
    products = far_and_pairs(pair_slots, far, table, own, sibling, near, passed)

    rows = channels // windows
    products = products.reshape(windows, slot_count * rows, 2 * channels).astype(jnp.float16)
    arrived = lax.all_to_all(products, "tm", 0, 0, tiled=True)
    total = jnp.sum(arrived.astype(jnp.float32), axis=0) * (4.0 / (samples * windows))
    return jnp.transpose(total.reshape(slot_count, rows, 2 * channels), (1, 0, 2))


def solution(mesh):
    return jax.shard_map(
        on_device,
        mesh=mesh,
        in_specs=(P("tm", "chan", None, None), P("chan", None)),
        out_specs=P("tm", "chan", None),
        check_vma=False,
    )
```

```python
import math

import jax
import jax.numpy as jnp
from jax import lax
from jax.experimental import pallas as pl
from jax.experimental.pallas import tpu as pltpu
from jax.sharding import PartitionSpec as P

LANES = 128
ROWS_PERIOD = 16
SPLIT = 32
GROUPS = 5
SLOTS_PER_STEP = 6
MIB = 1024 * 1024


def table_parts(samples):
    shape = (4 * SPLIT + samples // LANES * ROWS_PERIOD, LANES)
    row = lax.broadcasted_iota(jnp.int32, shape, 0)
    bin_low = lax.broadcasted_iota(jnp.int32, shape, 1) + 1
    part = row // SPLIT
    at = row % SPLIT
    step_row = row - 4 * SPLIT
    phases = jnp.where(
        part == 0,
        bin_low * at * SPLIT,
        jnp.where(
            part == 1,
            bin_low * at,
            jnp.where(
                part == 2,
                2 * SPLIT * at,
                jnp.where(part == 3, 2 * at, (step_row // ROWS_PERIOD) * (step_row % ROWS_PERIOD) * LANES),
            ),
        ),
    )
    angles = (phases % (2 * samples)).astype(jnp.float32) * (math.pi / samples)
    return jnp.cos(angles), jnp.sin(angles)


def whiten_bins(x, table, out_ref, bins):
    blocks, channels, samples = x.shape
    spectra = jnp.dot(x.reshape(blocks * channels, samples), table, preferred_element_type=jnp.float32)
    for block in range(blocks):
        part = spectra[block * channels : (block + 1) * channels]
        real, imag = part[:, :LANES], part[:, LANES:]
        power = jnp.sum(real * real + imag * imag, axis=0, keepdims=True) * (1.0 / channels)
        scale = 1.0 / jnp.sqrt(power + 1e-05)
        out_ref[block, :channels, bins] = (real * scale).astype(jnp.bfloat16)
        out_ref[block, channels:, bins] = (imag * scale).astype(jnp.bfloat16)


def first_kernel(cos_ref, sin_ref, x_ref, table_ref, out_ref, again_ref, low_cos_ref, low_sin_ref, sem):
    samples = x_ref.shape[2]
    fetch = pltpu.make_async_copy(x_ref, again_ref, sem)
    fetch.start()
    rows = lambda ref, part: ref[part * SPLIT : (part + 1) * SPLIT, :]
    for at in range(samples // SPLIT):
        high = lambda ref, part: ref[part * SPLIT + at : part * SPLIT + at + 1, :]
        taper = 0.5 - 0.5 * (high(cos_ref, 2) * rows(cos_ref, 3) - high(sin_ref, 2) * rows(sin_ref, 3))
        cos = high(cos_ref, 0) * rows(cos_ref, 1) - high(sin_ref, 0) * rows(sin_ref, 1)
        sin = high(sin_ref, 0) * rows(cos_ref, 1) + high(cos_ref, 0) * rows(sin_ref, 1)
        low_cos_ref[at * SPLIT : (at + 1) * SPLIT, :] = taper * cos
        low_sin_ref[at * SPLIT : (at + 1) * SPLIT, :] = taper * sin

    shape = (samples // ROWS_PERIOD, ROWS_PERIOD, LANES)
    for step in range(samples // LANES):
        low_cos = low_cos_ref[...].reshape(shape)
        low_sin = low_sin_ref[...].reshape(shape)
        step_rows = slice(4 * SPLIT + step * ROWS_PERIOD, 4 * SPLIT + (step + 1) * ROWS_PERIOD)
        step_cos = cos_ref[step_rows, :][None]
        step_sin = sin_ref[step_rows, :][None]
        real = low_cos * step_cos - low_sin * step_sin
        imag = -(low_sin * step_cos + low_cos * step_sin)
        columns = slice(2 * step * LANES, (2 * step + 1) * LANES)
        table_ref[:, columns] = real.reshape(samples, LANES).astype(jnp.bfloat16)
        columns = slice((2 * step + 1) * LANES, (2 * step + 2) * LANES)
        table_ref[:, columns] = imag.reshape(samples, LANES).astype(jnp.bfloat16)
    fetch.wait()
    whiten_all(again_ref, table_ref, out_ref)


def whiten_all(x_ref, table_ref, out_ref):
    x = x_ref[...]
    for step in range(x.shape[2] // LANES):
        table = table_ref[:, 2 * step * LANES : 2 * (step + 1) * LANES]
        whiten_bins(x, table, out_ref, slice(step * LANES, (step + 1) * LANES))


def hint(work):
    return pl.CostEstimate(flops=work, bytes_accessed=1 << 16, transcendentals=0)


def pinned(*arrays):
    return tuple(pltpu.with_memory_space_constraint(array, pltpu.VMEM) for array in arrays)


HERE = pl.BlockSpec(memory_space=pltpu.VMEM)


def whiten_first(x, parts):
    blocks, channels, samples = x.shape
    return pl.pallas_call(
        first_kernel,
        in_specs=[HERE, HERE, pl.BlockSpec(memory_space=pl.ANY)],
        out_specs=[HERE] * 3,
        out_shape=[
            pltpu.VMEM((samples, 2 * samples), jnp.bfloat16),
            pltpu.VMEM((blocks, 2 * channels, samples), jnp.bfloat16),
            pltpu.VMEM(x.shape, x.dtype),
        ],
        scratch_shapes=[pltpu.VMEM((samples, LANES), jnp.float32)] * 2 + [pltpu.SemaphoreType.DMA],
        compiler_params=pltpu.CompilerParams(vmem_limit_bytes=12 * MIB),
        cost_estimate=hint(blocks * channels * samples),
        name="table_and_own",
    )(*pinned(*parts), pltpu.with_memory_space_constraint(x, pltpu.HBM))


def whiten_next(x, table, name):
    blocks, channels, samples = x.shape
    return pl.pallas_call(
        whiten_all,
        in_specs=[HERE] * 2,
        out_specs=HERE,
        out_shape=pltpu.VMEM((blocks, 2 * channels, samples), jnp.bfloat16),
        compiler_params=pltpu.CompilerParams(vmem_limit_bytes=12 * MIB),
        cost_estimate=hint(17 * 10**9),
        name=name,
    )(*pinned(x, table))


def last_kernel(
    slots_ref, x_ref, table_ref, own_ref, sibling_ref, near_ref, passed_ref, out_ref, window_ref, sems
):
    step = pl.program_id(0)
    blocks, channels, samples = x_ref.shape

    @pl.when(step == 0)
    def _():
        parts = ((own_ref, 0), (sibling_ref, 1), (near_ref, 2), (passed_ref, 4))
        copies = [
            pltpu.make_async_copy(ref, window_ref.at[pl.ds(place * blocks, blocks)], sems.at[at])
            for at, (ref, place) in enumerate(parts)
        ]
        for copy in copies:
            copy.start()
        whiten_all(x_ref, table_ref, window_ref.at[pl.ds(3 * blocks, blocks)])
        for copy in copies:
            copy.wait()

    @pl.when(step > 0)
    def _():
        owner = lax.axis_index("chan")

        def place(block):
            block = jnp.where(block >= 0, block, owner * blocks)
            away = (lax.div(block, blocks) - owner) * (1 - 2 * lax.rem(owner, 2))
            return lax.rem(away + GROUPS, GROUPS) * blocks + lax.rem(block, blocks)

        found = []
        for at in range(SLOTS_PER_STEP):
            slot = (step - 1) * SLOTS_PER_STEP + at
            first, second = slots_ref[0, slot], slots_ref[1, slot]
            product = lax.dot_general(
                window_ref[place(first)],
                window_ref[place(second)],
                (((1,), (1,)), ((), ())),
                preferred_element_type=jnp.float32,
            )
            real = product[:channels, :channels] + product[channels:, channels:]
            imag = product[channels:, :channels] - product[:channels, channels:]
            live = jnp.where(first >= 0, 0.25, 0.0)
            both = jnp.concatenate([real, imag], axis=1) * live
            found.append(both.reshape(channels // 8, 8, 2 * channels))
        for pair in range(SLOTS_PER_STEP // 2):
            first, second = found[2 * pair], found[2 * pair + 1]
            row = lax.broadcasted_iota(jnp.int32, first.shape, 1)
            rows = slice(8 * pair, 8 * (pair + 1))
            out_ref[:, 0, rows] = jnp.where(row < 4, first, pltpu.roll(second, 4, 1))
            out_ref[:, 1, rows] = jnp.where(row < 4, pltpu.roll(first, 4, 1), second)


def far_and_pairs(slots, x, table, own, sibling, near, passed):
    blocks, channels, samples = x.shape
    slot_count = slots.shape[0]
    return pl.pallas_call(
        last_kernel,
        grid_spec=pltpu.PrefetchScalarGridSpec(
            num_scalar_prefetch=1,
            grid=(1 + slot_count // SLOTS_PER_STEP,),
            in_specs=[HERE] * 6,
            out_specs=pl.BlockSpec(
                (channels // 8, 2, 4 * SLOTS_PER_STEP, 2 * channels), lambda i, *_: (0, 0, jnp.maximum(i - 1, 0), 0)
            ),
            scratch_shapes=[
                pltpu.VMEM((GROUPS * blocks, 2 * channels, samples), jnp.bfloat16),
                pltpu.SemaphoreType.DMA((4,)),
            ],
        ),
        out_shape=pltpu.VMEM((channels // 8, 2, slot_count * 4, 2 * channels), jnp.float32),
        compiler_params=pltpu.CompilerParams(vmem_limit_bytes=20 * MIB),
        cost_estimate=hint(slot_count * channels * samples),
        name="far_and_pairs",
    )(slots.T, *pinned(x, table, own, sibling, near, passed))


def after_transfer(x, work, *others):
    anywhere = pl.BlockSpec(memory_space=pl.ANY)
    return pl.pallas_call(
        lambda x_ref, *refs: None,
        in_specs=[anywhere] * (1 + len(others)),
        out_specs=anywhere,
        out_shape=jax.ShapeDtypeStruct(x.shape, x.dtype),
        input_output_aliases={0: 0},
        compiler_params=pltpu.CompilerParams(vmem_limit_bytes=MIB),
        cost_estimate=hint(work),
        name="far_arrived",
    )(x, *others)


def on_device(strain, pair_slots):
    x = strain[0]
    blocks, channels, samples = x.shape
    owners = lax.axis_size("chan")
    windows = lax.axis_size("tm")
    slot_count = pair_slots.shape[0]
    even = range(0, owners, 2)
    odd = range(1, owners, 2)
    sibling_pairs = [(i, i ^ 1) for i in range(owners)]
    near_pairs = [((i + 2) % owners, i) for i in even] + [((i - 2) % owners, i) for i in odd]
    far_pairs = [((i - 2) % owners, i) for i in even] + [((i + 2) % owners, i) for i in odd]

    near = lax.ppermute(x, "chan", near_pairs)
    table, own, again = whiten_first(x, table_parts(samples))
    sibling = lax.ppermute(own, "chan", sibling_pairs)
    far = lax.ppermute(again, "chan", far_pairs)
    far = after_transfer(far, 100 * 10**9, sibling)
    near = whiten_next(near, table, "near")
    passed = lax.ppermute(near, "chan", sibling_pairs)
    products = far_and_pairs(pair_slots, far, table, own, sibling, near, passed)

    rows = channels // windows
    products = products.reshape(windows, slot_count * rows, 2 * channels).astype(jnp.float16)
    arrived = lax.all_to_all(products, "tm", 0, 0, tiled=True)
    total = jnp.sum(arrived.astype(jnp.float32), axis=0) * (4.0 / (samples * windows))
    return jnp.transpose(total.reshape(slot_count, rows, 2 * channels), (1, 0, 2))


def solution(mesh):
    return jax.shard_map(
        on_device,
        mesh=mesh,
        in_specs=(P("tm", "chan", None, None), P("chan", None)),
        out_specs=P("tm", "chan", None),
        check_vma=False,
    )
```

```python
import math

import jax
import jax.numpy as jnp
from jax import lax
from jax.experimental import pallas as pl
from jax.experimental.pallas import tpu as pltpu
from jax.sharding import PartitionSpec as P

LANES = 128
ROWS_PERIOD = 16
SPLIT = 32
GROUPS = 5
SLOTS_PER_STEP = 6
MIB = 1024 * 1024


def table_parts(samples):
    shape = (4 * SPLIT + samples // LANES * ROWS_PERIOD, LANES)
    row = lax.broadcasted_iota(jnp.int32, shape, 0)
    bin_low = lax.broadcasted_iota(jnp.int32, shape, 1) + 1
    part = row // SPLIT
    at = row % SPLIT
    step_row = row - 4 * SPLIT
    phases = jnp.where(
        part == 0,
        bin_low * at * SPLIT,
        jnp.where(
            part == 1,
            bin_low * at,
            jnp.where(
                part == 2,
                2 * SPLIT * at,
                jnp.where(part == 3, 2 * at, (step_row // ROWS_PERIOD) * (step_row % ROWS_PERIOD) * LANES),
            ),
        ),
    )
    angles = (phases % (2 * samples)).astype(jnp.float32) * (math.pi / samples)
    return jnp.cos(angles), jnp.sin(angles)


def whiten_bins(x, table, out_ref, bins):
    blocks, channels, samples = x.shape
    spectra = jnp.dot(x.reshape(blocks * channels, samples), table, preferred_element_type=jnp.float32)
    for block in range(blocks):
        part = spectra[block * channels : (block + 1) * channels]
        real, imag = part[:, :LANES], part[:, LANES:]
        power = jnp.sum(real * real + imag * imag, axis=0, keepdims=True) * (1.0 / channels)
        scale = 1.0 / jnp.sqrt(power + 1e-05)
        out_ref[block, :channels, bins] = (real * scale).astype(jnp.bfloat16)
        out_ref[block, channels:, bins] = (imag * scale).astype(jnp.bfloat16)


def first_kernel(cos_ref, sin_ref, x_ref, table_ref, out_ref, low_ref, high_ref, low_cos_ref, low_sin_ref, sems):
    blocks, _, samples = x_ref.shape
    half = blocks // 2
    fetches = [
        pltpu.make_async_copy(x_ref.at[:half], low_ref, sems.at[0]),
        pltpu.make_async_copy(x_ref.at[half:], high_ref, sems.at[1]),
    ]
    for fetch in fetches:
        fetch.start()
    rows = lambda ref, part: ref[part * SPLIT : (part + 1) * SPLIT, :]
    for at in range(samples // SPLIT):
        high = lambda ref, part: ref[part * SPLIT + at : part * SPLIT + at + 1, :]
        taper = 0.5 - 0.5 * (high(cos_ref, 2) * rows(cos_ref, 3) - high(sin_ref, 2) * rows(sin_ref, 3))
        cos = high(cos_ref, 0) * rows(cos_ref, 1) - high(sin_ref, 0) * rows(sin_ref, 1)
        sin = high(sin_ref, 0) * rows(cos_ref, 1) + high(cos_ref, 0) * rows(sin_ref, 1)
        low_cos_ref[at * SPLIT : (at + 1) * SPLIT, :] = taper * cos
        low_sin_ref[at * SPLIT : (at + 1) * SPLIT, :] = taper * sin

    shape = (samples // ROWS_PERIOD, ROWS_PERIOD, LANES)
    for step in range(samples // LANES):
        low_cos = low_cos_ref[...].reshape(shape)
        low_sin = low_sin_ref[...].reshape(shape)
        step_rows = slice(4 * SPLIT + step * ROWS_PERIOD, 4 * SPLIT + (step + 1) * ROWS_PERIOD)
        step_cos = cos_ref[step_rows, :][None]
        step_sin = sin_ref[step_rows, :][None]
        real = low_cos * step_cos - low_sin * step_sin
        imag = -(low_sin * step_cos + low_cos * step_sin)
        columns = slice(2 * step * LANES, (2 * step + 1) * LANES)
        table_ref[:, columns] = real.reshape(samples, LANES).astype(jnp.bfloat16)
        columns = slice((2 * step + 1) * LANES, (2 * step + 2) * LANES)
        table_ref[:, columns] = imag.reshape(samples, LANES).astype(jnp.bfloat16)
    for fetch in fetches:
        fetch.wait()
    whiten_all((low_ref, high_ref), table_ref, out_ref)


def whiten_all(x_refs, table_ref, out_ref):
    x = jnp.concatenate([x_ref[...] for x_ref in x_refs], axis=0)
    for step in range(x.shape[2] // LANES):
        table = table_ref[:, 2 * step * LANES : 2 * (step + 1) * LANES]
        whiten_bins(x, table, out_ref, slice(step * LANES, (step + 1) * LANES))


def hint(work):
    return pl.CostEstimate(flops=work, bytes_accessed=1 << 16, transcendentals=0)


def pinned(*arrays):
    return tuple(pltpu.with_memory_space_constraint(array, pltpu.VMEM) for array in arrays)


HERE = pl.BlockSpec(memory_space=pltpu.VMEM)


def whiten_first(x, parts):
    blocks, channels, samples = x.shape
    return pl.pallas_call(
        first_kernel,
        in_specs=[HERE, HERE, pl.BlockSpec(memory_space=pl.ANY)],
        out_specs=[HERE] * 4,
        out_shape=[
            pltpu.VMEM((samples, 2 * samples), jnp.bfloat16),
            pltpu.VMEM((blocks, 2 * channels, samples), jnp.bfloat16),
            pltpu.VMEM((blocks // 2, channels, samples), x.dtype),
            pltpu.VMEM((blocks // 2, channels, samples), x.dtype),
        ],
        scratch_shapes=[pltpu.VMEM((samples, LANES), jnp.float32)] * 2 + [pltpu.SemaphoreType.DMA((2,))],
        compiler_params=pltpu.CompilerParams(vmem_limit_bytes=12 * MIB),
        cost_estimate=hint(blocks * channels * samples),
        name="table_and_own",
    )(*pinned(*parts), pltpu.with_memory_space_constraint(x, pltpu.HBM))


def whiten_next(x, table, name):
    blocks, channels, samples = x.shape
    return pl.pallas_call(
        lambda x_ref, table_ref, out_ref: whiten_all((x_ref,), table_ref, out_ref),
        in_specs=[HERE] * 2,
        out_specs=HERE,
        out_shape=pltpu.VMEM((blocks, 2 * channels, samples), jnp.bfloat16),
        compiler_params=pltpu.CompilerParams(vmem_limit_bytes=12 * MIB),
        cost_estimate=hint(17 * 10**9),
        name=name,
    )(*pinned(x, table))


def last_kernel(
    slots_ref, low_ref, high_ref, table_ref, own_ref, sibling_ref, near_ref, passed_ref, out_ref, window_ref, sems
):
    step = pl.program_id(0)
    blocks, stacked, samples = own_ref.shape
    channels = stacked // 2

    @pl.when(step == 0)
    def _():
        parts = ((own_ref, 0), (sibling_ref, 1), (near_ref, 2), (passed_ref, 4))
        copies = [
            pltpu.make_async_copy(ref, window_ref.at[pl.ds(place * blocks, blocks)], sems.at[at])
            for at, (ref, place) in enumerate(parts)
        ]
        for copy in copies:
            copy.start()
        whiten_all((low_ref, high_ref), table_ref, window_ref.at[pl.ds(3 * blocks, blocks)])
        for copy in copies:
            copy.wait()

    @pl.when(step > 0)
    def _():
        owner = lax.axis_index("chan")

        def place(block):
            block = jnp.where(block >= 0, block, owner * blocks)
            away = (lax.div(block, blocks) - owner) * (1 - 2 * lax.rem(owner, 2))
            return lax.rem(away + GROUPS, GROUPS) * blocks + lax.rem(block, blocks)

        found = []
        for at in range(SLOTS_PER_STEP):
            slot = (step - 1) * SLOTS_PER_STEP + at
            first, second = slots_ref[0, slot], slots_ref[1, slot]
            product = lax.dot_general(
                window_ref[place(first)],
                window_ref[place(second)],
                (((1,), (1,)), ((), ())),
                preferred_element_type=jnp.float32,
            )
            real = product[:channels, :channels] + product[channels:, channels:]
            imag = product[channels:, :channels] - product[:channels, channels:]
            live = jnp.where(first >= 0, 0.25, 0.0)
            both = jnp.concatenate([real, imag], axis=1) * live
            found.append(both.reshape(channels // 8, 8, 2 * channels))
        for pair in range(SLOTS_PER_STEP // 2):
            first, second = found[2 * pair], found[2 * pair + 1]
            row = lax.broadcasted_iota(jnp.int32, first.shape, 1)
            rows = slice(8 * pair, 8 * (pair + 1))
            out_ref[:, 0, rows] = jnp.where(row < 4, first, pltpu.roll(second, 4, 1))
            out_ref[:, 1, rows] = jnp.where(row < 4, pltpu.roll(first, 4, 1), second)


def far_and_pairs(slots, low, high, table, own, sibling, near, passed):
    blocks, stacked, samples = own.shape
    channels = stacked // 2
    slot_count = slots.shape[0]
    return pl.pallas_call(
        last_kernel,
        grid_spec=pltpu.PrefetchScalarGridSpec(
            num_scalar_prefetch=1,
            grid=(1 + slot_count // SLOTS_PER_STEP,),
            in_specs=[HERE] * 7,
            out_specs=pl.BlockSpec(
                (channels // 8, 2, 4 * SLOTS_PER_STEP, 2 * channels), lambda i, *_: (0, 0, jnp.maximum(i - 1, 0), 0)
            ),
            scratch_shapes=[
                pltpu.VMEM((GROUPS * blocks, 2 * channels, samples), jnp.bfloat16),
                pltpu.SemaphoreType.DMA((4,)),
            ],
        ),
        out_shape=pltpu.VMEM((channels // 8, 2, slot_count * 4, 2 * channels), jnp.float32),
        compiler_params=pltpu.CompilerParams(vmem_limit_bytes=20 * MIB),
        cost_estimate=hint(slot_count * channels * samples),
        name="far_and_pairs",
    )(slots.T, *pinned(low, high, table, own, sibling, near, passed))


def after_transfer(x, work, *others):
    anywhere = pl.BlockSpec(memory_space=pl.ANY)
    return pl.pallas_call(
        lambda x_ref, *refs: None,
        in_specs=[anywhere] * (1 + len(others)),
        out_specs=anywhere,
        out_shape=jax.ShapeDtypeStruct(x.shape, x.dtype),
        input_output_aliases={0: 0},
        compiler_params=pltpu.CompilerParams(vmem_limit_bytes=MIB),
        cost_estimate=hint(work),
        name="far_arrived",
    )(x, *others)


def on_device(strain, pair_slots):
    x = strain[0]
    blocks, channels, samples = x.shape
    owners = lax.axis_size("chan")
    windows = lax.axis_size("tm")
    slot_count = pair_slots.shape[0]
    even = range(0, owners, 2)
    odd = range(1, owners, 2)
    sibling_pairs = [(i, i ^ 1) for i in range(owners)]
    near_pairs = [((i + 2) % owners, i) for i in even] + [((i - 2) % owners, i) for i in odd]
    far_pairs = [((i - 2) % owners, i) for i in even] + [((i + 2) % owners, i) for i in odd]

    near = lax.ppermute(x, "chan", near_pairs)
    table, own, low, high = whiten_first(x, table_parts(samples))
    sibling = lax.ppermute(own, "chan", sibling_pairs)
    low, high = [lax.ppermute(part, "chan", far_pairs) for part in (low, high)]
    low = after_transfer(low, 100 * 10**9, high, sibling)
    near = whiten_next(near, table, "near")
    passed = lax.ppermute(near, "chan", sibling_pairs)
    products = far_and_pairs(pair_slots, low, high, table, own, sibling, near, passed)

    rows = channels // windows
    products = products.reshape(windows, slot_count * rows, 2 * channels).astype(jnp.float16)
    arrived = lax.all_to_all(products, "tm", 0, 0, tiled=True)
    total = jnp.sum(arrived.astype(jnp.float32), axis=0) * (4.0 / (samples * windows))
    return jnp.transpose(total.reshape(slot_count, rows, 2 * channels), (1, 0, 2))


def solution(mesh):
    return jax.shard_map(
        on_device,
        mesh=mesh,
        in_specs=(P("tm", "chan", None, None), P("chan", None)),
        out_specs=P("tm", "chan", None),
        check_vma=False,
    )
```

```python
import functools
import math

import jax
import jax.numpy as jnp
from jax import lax
from jax.experimental import pallas as pl
from jax.experimental.pallas import tpu as pltpu
from jax.sharding import PartitionSpec as P

LANES = 128
ROWS_PERIOD = 16
SPLIT = 32
GROUPS = 5
SLOTS_PER_STEP = 6
SLOTS_PER_GROUP = 2
MIB = 1024 * 1024


def table_parts(samples):
    shape = (4 * SPLIT + samples // LANES * ROWS_PERIOD, LANES)
    row = lax.broadcasted_iota(jnp.int32, shape, 0)
    bin_low = lax.broadcasted_iota(jnp.int32, shape, 1) + 1
    part = row // SPLIT
    at = row % SPLIT
    step_row = row - 4 * SPLIT
    phases = jnp.where(
        part == 0,
        bin_low * at * SPLIT,
        jnp.where(
            part == 1,
            bin_low * at,
            jnp.where(
                part == 2,
                2 * SPLIT * at,
                jnp.where(part == 3, 2 * at, (step_row // ROWS_PERIOD) * (step_row % ROWS_PERIOD) * LANES),
            ),
        ),
    )
    angles = (phases % (2 * samples)).astype(jnp.float32) * (math.pi / samples)
    return jnp.cos(angles), jnp.sin(angles)


def whiten_bins(x, table, out_ref, bins):
    blocks, channels, samples = x.shape
    spectra = jnp.dot(x.reshape(blocks * channels, samples), table, preferred_element_type=jnp.float32)
    for block in range(blocks):
        part = spectra[block * channels : (block + 1) * channels]
        real, imag = part[:, :LANES], part[:, LANES:]
        power = jnp.sum(real * real + imag * imag, axis=0, keepdims=True) * (1.0 / channels)
        scale = 1.0 / jnp.sqrt(power + 1e-05)
        out_ref[block, :channels, bins] = (real * scale).astype(jnp.bfloat16)
        out_ref[block, channels:, bins] = (imag * scale).astype(jnp.bfloat16)


def first_kernel(cos_ref, sin_ref, x_ref, table_ref, out_ref, again_ref, low_cos_ref, low_sin_ref, sem):
    samples = x_ref.shape[2]
    fetch = pltpu.make_async_copy(x_ref, again_ref, sem)
    fetch.start()
    rows = lambda ref, part: ref[part * SPLIT : (part + 1) * SPLIT, :]
    for at in range(samples // SPLIT):
        high = lambda ref, part: ref[part * SPLIT + at : part * SPLIT + at + 1, :]
        taper = 0.5 - 0.5 * (high(cos_ref, 2) * rows(cos_ref, 3) - high(sin_ref, 2) * rows(sin_ref, 3))
        cos = high(cos_ref, 0) * rows(cos_ref, 1) - high(sin_ref, 0) * rows(sin_ref, 1)
        sin = high(sin_ref, 0) * rows(cos_ref, 1) + high(cos_ref, 0) * rows(sin_ref, 1)
        low_cos_ref[at * SPLIT : (at + 1) * SPLIT, :] = taper * cos
        low_sin_ref[at * SPLIT : (at + 1) * SPLIT, :] = taper * sin

    shape = (samples // ROWS_PERIOD, ROWS_PERIOD, LANES)
    for step in range(samples // LANES):
        low_cos = low_cos_ref[...].reshape(shape)
        low_sin = low_sin_ref[...].reshape(shape)
        step_rows = slice(4 * SPLIT + step * ROWS_PERIOD, 4 * SPLIT + (step + 1) * ROWS_PERIOD)
        step_cos = cos_ref[step_rows, :][None]
        step_sin = sin_ref[step_rows, :][None]
        real = low_cos * step_cos - low_sin * step_sin
        imag = -(low_sin * step_cos + low_cos * step_sin)
        columns = slice(2 * step * LANES, (2 * step + 1) * LANES)
        table_ref[:, columns] = real.reshape(samples, LANES).astype(jnp.bfloat16)
        columns = slice((2 * step + 1) * LANES, (2 * step + 2) * LANES)
        table_ref[:, columns] = imag.reshape(samples, LANES).astype(jnp.bfloat16)
    fetch.wait()
    whiten_all(again_ref, table_ref, out_ref)


def whiten_all(x_ref, table_ref, out_ref):
    x = x_ref[...]
    for step in range(x.shape[2] // LANES):
        table = table_ref[:, 2 * step * LANES : 2 * (step + 1) * LANES]
        whiten_bins(x, table, out_ref, slice(step * LANES, (step + 1) * LANES))


def hint(work):
    return pl.CostEstimate(flops=work, bytes_accessed=1 << 16, transcendentals=0)


def pinned(*arrays):
    return tuple(pltpu.with_memory_space_constraint(array, pltpu.VMEM) for array in arrays)


HERE = pl.BlockSpec(memory_space=pltpu.VMEM)


def whiten_first(x, parts):
    blocks, channels, samples = x.shape
    return pl.pallas_call(
        first_kernel,
        in_specs=[HERE, HERE, pl.BlockSpec(memory_space=pl.ANY)],
        out_specs=[HERE] * 3,
        out_shape=[
            pltpu.VMEM((samples, 2 * samples), jnp.bfloat16),
            pltpu.VMEM((blocks, 2 * channels, samples), jnp.bfloat16),
            pltpu.VMEM(x.shape, x.dtype),
        ],
        scratch_shapes=[pltpu.VMEM((samples, LANES), jnp.float32)] * 2 + [pltpu.SemaphoreType.DMA],
        compiler_params=pltpu.CompilerParams(vmem_limit_bytes=12 * MIB),
        cost_estimate=hint(blocks * channels * samples),
        name="table_and_own",
    )(*pinned(*parts), pltpu.with_memory_space_constraint(x, pltpu.HBM))


def whiten_next(x, table, name):
    blocks, channels, samples = x.shape
    return pl.pallas_call(
        whiten_all,
        in_specs=[HERE] * 2,
        out_specs=HERE,
        out_shape=pltpu.VMEM((blocks, 2 * channels, samples), jnp.bfloat16),
        compiler_params=pltpu.CompilerParams(vmem_limit_bytes=12 * MIB),
        cost_estimate=hint(17 * 10**9),
        name=name,
    )(*pinned(x, table))


def last_kernel(
    slots_ref, x_ref, table_ref, own_ref, sibling_ref, near_ref, passed_ref, out_ref, group_ref, window_ref, sems
):
    step = pl.program_id(0)
    blocks, channels, samples = x_ref.shape

    @pl.when(step == 0)
    def _():
        parts = ((own_ref, 0), (sibling_ref, 1), (near_ref, 2), (passed_ref, 4))
        copies = [
            pltpu.make_async_copy(ref, window_ref.at[pl.ds(place * blocks, blocks)], sems.at[at])
            for at, (ref, place) in enumerate(parts)
        ]
        for copy in copies:
            copy.start()
        whiten_all(x_ref, table_ref, window_ref.at[pl.ds(3 * blocks, blocks)])
        for copy in copies:
            copy.wait()

    group_ref[0] = sum(
        (slots_ref[0, slot] >= 0).astype(jnp.int32) for slot in range(SLOTS_PER_GROUP, slots_ref.shape[1], SLOTS_PER_GROUP)
    )

    @pl.when((step > 0) & (slots_ref[0, jnp.maximum(step - 1, 0) * SLOTS_PER_STEP] >= 0))
    def _():
        owner = lax.axis_index("chan")

        def place(block):
            block = jnp.where(block >= 0, block, owner * blocks)
            away = (lax.div(block, blocks) - owner) * (1 - 2 * lax.rem(owner, 2))
            return lax.rem(away + GROUPS, GROUPS) * blocks + lax.rem(block, blocks)

        found = []
        for at in range(SLOTS_PER_STEP):
            slot = (step - 1) * SLOTS_PER_STEP + at
            first, second = slots_ref[0, slot], slots_ref[1, slot]
            product = lax.dot_general(
                window_ref[place(first)],
                window_ref[place(second)],
                (((1,), (1,)), ((), ())),
                preferred_element_type=jnp.float32,
            )
            real = product[:channels, :channels] + product[channels:, channels:]
            imag = product[channels:, :channels] - product[:channels, channels:]
            live = jnp.where(first >= 0, 0.25, 0.0)
            both = jnp.concatenate([real, imag], axis=1) * live
            found.append(both.reshape(channels // 8, 8, 2 * channels))
        for pair in range(SLOTS_PER_STEP // 2):
            first, second = found[2 * pair], found[2 * pair + 1]
            row = lax.broadcasted_iota(jnp.int32, first.shape, 1)
            rows = slice(8 * pair, 8 * (pair + 1))
            out_ref[:, 0, rows] = jnp.where(row < 4, first, pltpu.roll(second, 4, 1))
            out_ref[:, 1, rows] = jnp.where(row < 4, pltpu.roll(first, 4, 1), second)


def far_and_pairs(slots, x, table, own, sibling, near, passed):
    blocks, channels, samples = x.shape
    slot_count = slots.shape[0]
    return pl.pallas_call(
        last_kernel,
        grid_spec=pltpu.PrefetchScalarGridSpec(
            num_scalar_prefetch=1,
            grid=(1 + slot_count // SLOTS_PER_STEP,),
            in_specs=[HERE] * 6,
            out_specs=[
                pl.BlockSpec(
                    (channels // 8, 2, 4 * SLOTS_PER_STEP, 2 * channels),
                    lambda i, *_: (0, 0, jnp.maximum(i - 1, 0), 0),
                ),
                pl.BlockSpec(memory_space=pltpu.SMEM),
            ],
            scratch_shapes=[
                pltpu.VMEM((GROUPS * blocks, 2 * channels, samples), jnp.bfloat16),
                pltpu.SemaphoreType.DMA((4,)),
            ],
        ),
        out_shape=[
            jax.ShapeDtypeStruct((channels // 8, 2, slot_count * 4, 2 * channels), jnp.float32),
            jax.ShapeDtypeStruct((1,), jnp.int32),
        ],
        compiler_params=pltpu.CompilerParams(vmem_limit_bytes=20 * MIB),
        cost_estimate=hint(slot_count * channels * samples),
        name="far_and_pairs",
    )(slots.T, *pinned(x, table, own, sibling, near, passed))


def after_transfer(x, work, *others):
    anywhere = pl.BlockSpec(memory_space=pl.ANY)
    return pl.pallas_call(
        lambda x_ref, *refs: None,
        in_specs=[anywhere] * (1 + len(others)),
        out_specs=anywhere,
        out_shape=jax.ShapeDtypeStruct(x.shape, x.dtype),
        input_output_aliases={0: 0},
        compiler_params=pltpu.CompilerParams(vmem_limit_bytes=MIB),
        cost_estimate=hint(work),
        name="far_arrived",
    )(x, *others)


def on_device(strain, pair_slots):
    x = strain[0]
    blocks, channels, samples = x.shape
    owners = lax.axis_size("chan")
    windows = lax.axis_size("tm")
    slot_count = pair_slots.shape[0]
    even = range(0, owners, 2)
    odd = range(1, owners, 2)
    sibling_pairs = [(i, i ^ 1) for i in range(owners)]
    near_pairs = [((i + 2) % owners, i) for i in even] + [((i - 2) % owners, i) for i in odd]
    far_pairs = [((i - 2) % owners, i) for i in even] + [((i + 2) % owners, i) for i in odd]

    near = lax.ppermute(x, "chan", near_pairs)
    table, own, again = whiten_first(x, table_parts(samples))
    sibling = lax.ppermute(own, "chan", sibling_pairs)
    far = lax.ppermute(again, "chan", far_pairs)
    far = after_transfer(far, 100 * 10**9, sibling)
    near = whiten_next(near, table, "near")
    passed = lax.ppermute(near, "chan", sibling_pairs)
    products, group = far_and_pairs(pair_slots, far, table, own, sibling, near, passed)

    rows = channels // windows
    products = products.reshape(windows, slot_count * rows, 2 * channels)

    def summed(slots, products):
        sent = products[:, : slots * rows].astype(jnp.float16)
        arrived = lax.all_to_all(sent, "tm", 0, 0, tiled=True)
        total = jnp.sum(arrived.astype(jnp.float32), axis=0) * (4.0 / (samples * windows))
        return jnp.pad(total, ((0, (slot_count - slots) * rows), (0, 0)))

    total = lax.switch(
        group[0],
        [functools.partial(summed, slots) for slots in range(SLOTS_PER_GROUP, slot_count + 1, SLOTS_PER_GROUP)],
        products,
    )
    return jnp.transpose(total.reshape(slot_count, rows, 2 * channels), (1, 0, 2))


def solution(mesh):
    return jax.shard_map(
        on_device,
        mesh=mesh,
        in_specs=(P("tm", "chan", None, None), P("chan", None)),
        out_specs=P("tm", "chan", None),
        check_vma=False,
    )
```

```python
import functools
import math

import jax
import jax.numpy as jnp
from jax import lax
from jax.experimental import pallas as pl
from jax.experimental.pallas import tpu as pltpu
from jax.sharding import PartitionSpec as P

LANES = 128
ROWS_PERIOD = 16
SPLIT = 32
GROUPS = 5
SLOTS_PER_STEP = 6
SLOTS_PER_GROUP = 2
MIB = 1024 * 1024


def table_parts(samples):
    shape = (4 * SPLIT + samples // LANES * ROWS_PERIOD, LANES)
    row = lax.broadcasted_iota(jnp.int32, shape, 0)
    bin_low = lax.broadcasted_iota(jnp.int32, shape, 1) + 1
    part = row // SPLIT
    at = row % SPLIT
    step_row = row - 4 * SPLIT
    phases = jnp.where(
        part == 0,
        bin_low * at * SPLIT,
        jnp.where(
            part == 1,
            bin_low * at,
            jnp.where(
                part == 2,
                2 * SPLIT * at,
                jnp.where(part == 3, 2 * at, (step_row // ROWS_PERIOD) * (step_row % ROWS_PERIOD) * LANES),
            ),
        ),
    )
    angles = (phases % (2 * samples)).astype(jnp.float32) * (math.pi / samples)
    return jnp.cos(angles), jnp.sin(angles)


def whiten_bins(x, table, out_ref, bins):
    blocks, channels, samples = x.shape
    spectra = jnp.dot(x.reshape(blocks * channels, samples), table, preferred_element_type=jnp.float32)
    for block in range(blocks):
        part = spectra[block * channels : (block + 1) * channels]
        real, imag = part[:, :LANES], part[:, LANES:]
        power = jnp.sum(real * real + imag * imag, axis=0, keepdims=True) * (1.0 / channels)
        scale = 1.0 / jnp.sqrt(power + 1e-05)
        out_ref[block, :channels, bins] = (real * scale).astype(jnp.bfloat16)
        out_ref[block, channels:, bins] = (imag * scale).astype(jnp.bfloat16)


def first_kernel(cos_ref, sin_ref, x_ref, table_ref, out_ref, again_ref, low_cos_ref, low_sin_ref, sem):
    samples = x_ref.shape[2]
    fetch = pltpu.make_async_copy(x_ref, again_ref, sem)
    fetch.start()
    rows = lambda ref, part: ref[part * SPLIT : (part + 1) * SPLIT, :]
    for at in range(samples // SPLIT):
        high = lambda ref, part: ref[part * SPLIT + at : part * SPLIT + at + 1, :]
        taper = 0.5 - 0.5 * (high(cos_ref, 2) * rows(cos_ref, 3) - high(sin_ref, 2) * rows(sin_ref, 3))
        cos = high(cos_ref, 0) * rows(cos_ref, 1) - high(sin_ref, 0) * rows(sin_ref, 1)
        sin = high(sin_ref, 0) * rows(cos_ref, 1) + high(cos_ref, 0) * rows(sin_ref, 1)
        low_cos_ref[at * SPLIT : (at + 1) * SPLIT, :] = taper * cos
        low_sin_ref[at * SPLIT : (at + 1) * SPLIT, :] = taper * sin

    shape = (samples // ROWS_PERIOD, ROWS_PERIOD, LANES)
    for step in range(samples // LANES):
        low_cos = low_cos_ref[...].reshape(shape)
        low_sin = low_sin_ref[...].reshape(shape)
        step_rows = slice(4 * SPLIT + step * ROWS_PERIOD, 4 * SPLIT + (step + 1) * ROWS_PERIOD)
        step_cos = cos_ref[step_rows, :][None]
        step_sin = sin_ref[step_rows, :][None]
        real = low_cos * step_cos - low_sin * step_sin
        imag = -(low_sin * step_cos + low_cos * step_sin)
        columns = slice(2 * step * LANES, (2 * step + 1) * LANES)
        table_ref[:, columns] = real.reshape(samples, LANES).astype(jnp.bfloat16)
        columns = slice((2 * step + 1) * LANES, (2 * step + 2) * LANES)
        table_ref[:, columns] = imag.reshape(samples, LANES).astype(jnp.bfloat16)
    fetch.wait()
    whiten_all(again_ref, table_ref, out_ref)


def whiten_all(x_ref, table_ref, out_ref):
    x = x_ref[...]
    for step in range(x.shape[2] // LANES):
        table = table_ref[:, 2 * step * LANES : 2 * (step + 1) * LANES]
        whiten_bins(x, table, out_ref, slice(step * LANES, (step + 1) * LANES))


def hint(work):
    return pl.CostEstimate(flops=work, bytes_accessed=1 << 16, transcendentals=0)


def pinned(*arrays):
    return tuple(pltpu.with_memory_space_constraint(array, pltpu.VMEM) for array in arrays)


HERE = pl.BlockSpec(memory_space=pltpu.VMEM)


def whiten_first(x, parts):
    blocks, channels, samples = x.shape
    return pl.pallas_call(
        first_kernel,
        in_specs=[HERE, HERE, pl.BlockSpec(memory_space=pl.ANY)],
        out_specs=[HERE] * 3,
        out_shape=[
            pltpu.VMEM((samples, 2 * samples), jnp.bfloat16),
            pltpu.VMEM((blocks, 2 * channels, samples), jnp.bfloat16),
            pltpu.VMEM(x.shape, x.dtype),
        ],
        scratch_shapes=[pltpu.VMEM((samples, LANES), jnp.float32)] * 2 + [pltpu.SemaphoreType.DMA],
        compiler_params=pltpu.CompilerParams(vmem_limit_bytes=12 * MIB),
        cost_estimate=hint(blocks * channels * samples),
        name="table_and_own",
    )(*pinned(*parts), pltpu.with_memory_space_constraint(x, pltpu.HBM))


def whiten_next(x, table, name):
    blocks, channels, samples = x.shape
    return pl.pallas_call(
        whiten_all,
        in_specs=[HERE] * 2,
        out_specs=HERE,
        out_shape=pltpu.VMEM((blocks, 2 * channels, samples), jnp.bfloat16),
        compiler_params=pltpu.CompilerParams(vmem_limit_bytes=12 * MIB),
        cost_estimate=hint(17 * 10**9),
        name=name,
    )(*pinned(x, table))


def last_kernel(
    slots_ref, x_ref, table_ref, own_ref, sibling_ref, near_ref, passed_ref, out_ref, group_ref, window_ref, sems
):
    step = pl.program_id(0)
    blocks, channels, samples = x_ref.shape

    @pl.when(step == 0)
    def _():
        parts = ((own_ref, 0), (sibling_ref, 1), (near_ref, 2), (passed_ref, 4))
        copies = [
            pltpu.make_async_copy(ref, window_ref.at[pl.ds(place * blocks, blocks)], sems.at[at])
            for at, (ref, place) in enumerate(parts)
        ]
        for copy in copies:
            copy.start()
        whiten_all(x_ref, table_ref, window_ref.at[pl.ds(3 * blocks, blocks)])
        for copy in copies:
            copy.wait()

    group_ref[0] = sum(
        (slots_ref[0, slot] >= 0).astype(jnp.int32) for slot in range(SLOTS_PER_GROUP, slots_ref.shape[1], SLOTS_PER_GROUP)
    )

    @pl.when((step > 0) & (slots_ref[0, jnp.maximum(step - 1, 0) * SLOTS_PER_STEP] >= 0))
    def _():
        owner = lax.axis_index("chan")

        def place(block):
            block = jnp.where(block >= 0, block, owner * blocks)
            away = (lax.div(block, blocks) - owner) * (1 - 2 * lax.rem(owner, 2))
            return lax.rem(away + GROUPS, GROUPS) * blocks + lax.rem(block, blocks)

        found = []
        for at in range(SLOTS_PER_STEP):
            slot = (step - 1) * SLOTS_PER_STEP + at
            first, second = slots_ref[0, slot], slots_ref[1, slot]
            product = lax.dot_general(
                window_ref[place(first)],
                window_ref[place(second)],
                (((1,), (1,)), ((), ())),
                preferred_element_type=jnp.float32,
            )
            real = product[:channels, :channels] + product[channels:, channels:]
            imag = product[channels:, :channels] - product[:channels, channels:]
            live = jnp.where(first >= 0, 0.25, 0.0)
            both = jnp.concatenate([real, imag], axis=1) * live
            found.append(both.reshape(channels // 8, 8, 2 * channels))
        for pair in range(SLOTS_PER_STEP // 2):
            first, second = found[2 * pair], found[2 * pair + 1]
            row = lax.broadcasted_iota(jnp.int32, first.shape, 1)
            rows = slice(8 * pair, 8 * (pair + 1))
            out_ref[:, 0, rows] = jnp.where(row < 4, first, pltpu.roll(second, 4, 1))
            out_ref[:, 1, rows] = jnp.where(row < 4, pltpu.roll(first, 4, 1), second)


def far_and_pairs(slots, x, table, own, sibling, near, passed):
    blocks, channels, samples = x.shape
    slot_count = slots.shape[0]
    return pl.pallas_call(
        last_kernel,
        grid_spec=pltpu.PrefetchScalarGridSpec(
            num_scalar_prefetch=1,
            grid=(1 + slot_count // SLOTS_PER_STEP,),
            in_specs=[HERE] * 6,
            out_specs=[
                pl.BlockSpec(
                    (channels // 8, 2, 4 * SLOTS_PER_STEP, 2 * channels),
                    lambda i, *_: (0, 0, jnp.maximum(i - 1, 0), 0),
                ),
                pl.BlockSpec(memory_space=pltpu.SMEM),
            ],
            scratch_shapes=[
                pltpu.VMEM((GROUPS * blocks, 2 * channels, samples), jnp.bfloat16),
                pltpu.SemaphoreType.DMA((4,)),
            ],
        ),
        out_shape=[
            jax.ShapeDtypeStruct((channels // 8, 2, slot_count * 4, 2 * channels), jnp.float32),
            jax.ShapeDtypeStruct((1,), jnp.int32),
        ],
        compiler_params=pltpu.CompilerParams(vmem_limit_bytes=20 * MIB),
        cost_estimate=hint(slot_count * channels * samples),
        name="far_and_pairs",
    )(slots.T, *pinned(x, table, own, sibling, near, passed))


def after_transfer(x, work, *others):
    anywhere = pl.BlockSpec(memory_space=pl.ANY)
    return pl.pallas_call(
        lambda x_ref, *refs: None,
        in_specs=[anywhere] * (1 + len(others)),
        out_specs=anywhere,
        out_shape=jax.ShapeDtypeStruct(x.shape, x.dtype),
        input_output_aliases={0: 0},
        compiler_params=pltpu.CompilerParams(vmem_limit_bytes=MIB),
        cost_estimate=hint(work),
        name="far_arrived",
    )(x, *others)


def on_device(strain, pair_slots):
    x = strain[0]
    blocks, channels, samples = x.shape
    owners = lax.axis_size("chan")
    windows = lax.axis_size("tm")
    slot_count = pair_slots.shape[0]
    even = range(0, owners, 2)
    odd = range(1, owners, 2)
    sibling_pairs = [(i, i ^ 1) for i in range(owners)]
    inside = lambda pairs: [(source, target) for source, target in pairs if 0 <= source < owners]
    near_pairs = inside([(i + 2, i) for i in even] + [(i - 2, i) for i in odd])
    far_pairs = inside([(i - 2, i) for i in even] + [(i + 2, i) for i in odd])

    near = lax.ppermute(x, "chan", near_pairs)
    table, own, again = whiten_first(x, table_parts(samples))
    sibling = lax.ppermute(own, "chan", sibling_pairs)
    far = lax.ppermute(again, "chan", far_pairs)
    far = after_transfer(far, 100 * 10**9, sibling)
    near = whiten_next(near, table, "near")
    passed = lax.ppermute(near, "chan", sibling_pairs)
    products, group = far_and_pairs(pair_slots, far, table, own, sibling, near, passed)

    rows = channels // windows
    products = products.reshape(windows, slot_count * rows, 2 * channels)

    def summed(slots, products):
        sent = products[:, : slots * rows].astype(jnp.float16)
        arrived = lax.all_to_all(sent, "tm", 0, 0, tiled=True)
        total = jnp.sum(arrived.astype(jnp.float32), axis=0) * (4.0 / (samples * windows))
        return jnp.pad(total, ((0, (slot_count - slots) * rows), (0, 0)))

    total = lax.switch(
        group[0],
        [functools.partial(summed, slots) for slots in range(SLOTS_PER_GROUP, slot_count + 1, SLOTS_PER_GROUP)],
        products,
    )
    return jnp.transpose(total.reshape(slot_count, rows, 2 * channels), (1, 0, 2))


def solution(mesh):
    return jax.shard_map(
        on_device,
        mesh=mesh,
        in_specs=(P("tm", "chan", None, None), P("chan", None)),
        out_specs=P("tm", "chan", None),
        check_vma=False,
    )
```

```python
import functools
import math

import jax
import jax.numpy as jnp
from jax import lax
from jax.experimental import pallas as pl
from jax.experimental.pallas import tpu as pltpu
from jax.sharding import PartitionSpec as P

LANES = 128
ROWS_PERIOD = 16
SPLIT = 32
GROUPS = 5
SLOTS_PER_STEP = 4
SLOTS_PER_GROUP = 2
MIB = 1024 * 1024


def table_parts(samples):
    shape = (4 * SPLIT + samples // LANES * ROWS_PERIOD, LANES)
    row = lax.broadcasted_iota(jnp.int32, shape, 0)
    bin_low = lax.broadcasted_iota(jnp.int32, shape, 1) + 1
    part = row // SPLIT
    at = row % SPLIT
    step_row = row - 4 * SPLIT
    phases = jnp.where(
        part == 0,
        bin_low * at * SPLIT,
        jnp.where(
            part == 1,
            bin_low * at,
            jnp.where(
                part == 2,
                2 * SPLIT * at,
                jnp.where(part == 3, 2 * at, (step_row // ROWS_PERIOD) * (step_row % ROWS_PERIOD) * LANES),
            ),
        ),
    )
    angles = (phases % (2 * samples)).astype(jnp.float32) * (math.pi / samples)
    return jnp.cos(angles), jnp.sin(angles)


def whiten_bins(x, table, out_ref, bins):
    blocks, channels, samples = x.shape
    spectra = jnp.dot(x.reshape(blocks * channels, samples), table, preferred_element_type=jnp.float32)
    for block in range(blocks):
        part = spectra[block * channels : (block + 1) * channels]
        real, imag = part[:, :LANES], part[:, LANES:]
        power = jnp.sum(real * real + imag * imag, axis=0, keepdims=True) * (1.0 / channels)
        scale = 1.0 / jnp.sqrt(power + 1e-05)
        out_ref[block, :channels, bins] = (real * scale).astype(jnp.bfloat16)
        out_ref[block, channels:, bins] = (imag * scale).astype(jnp.bfloat16)


def first_kernel(cos_ref, sin_ref, x_ref, table_ref, out_ref, again_ref, low_cos_ref, low_sin_ref, sem):
    samples = x_ref.shape[2]
    fetch = pltpu.make_async_copy(x_ref, again_ref, sem)
    fetch.start()
    rows = lambda ref, part: ref[part * SPLIT : (part + 1) * SPLIT, :]
    for at in range(samples // SPLIT):
        high = lambda ref, part: ref[part * SPLIT + at : part * SPLIT + at + 1, :]
        taper = 0.5 - 0.5 * (high(cos_ref, 2) * rows(cos_ref, 3) - high(sin_ref, 2) * rows(sin_ref, 3))
        cos = high(cos_ref, 0) * rows(cos_ref, 1) - high(sin_ref, 0) * rows(sin_ref, 1)
        sin = high(sin_ref, 0) * rows(cos_ref, 1) + high(cos_ref, 0) * rows(sin_ref, 1)
        low_cos_ref[at * SPLIT : (at + 1) * SPLIT, :] = taper * cos
        low_sin_ref[at * SPLIT : (at + 1) * SPLIT, :] = taper * sin

    shape = (samples // ROWS_PERIOD, ROWS_PERIOD, LANES)
    for step in range(samples // LANES):
        low_cos = low_cos_ref[...].reshape(shape)
        low_sin = low_sin_ref[...].reshape(shape)
        step_rows = slice(4 * SPLIT + step * ROWS_PERIOD, 4 * SPLIT + (step + 1) * ROWS_PERIOD)
        step_cos = cos_ref[step_rows, :][None]
        step_sin = sin_ref[step_rows, :][None]
        real = low_cos * step_cos - low_sin * step_sin
        imag = -(low_sin * step_cos + low_cos * step_sin)
        columns = slice(2 * step * LANES, (2 * step + 1) * LANES)
        table_ref[:, columns] = real.reshape(samples, LANES).astype(jnp.bfloat16)
        columns = slice((2 * step + 1) * LANES, (2 * step + 2) * LANES)
        table_ref[:, columns] = imag.reshape(samples, LANES).astype(jnp.bfloat16)
    fetch.wait()
    whiten_all(again_ref, table_ref, out_ref)


def whiten_all(x_ref, table_ref, out_ref):
    x = x_ref[...]
    for step in range(x.shape[2] // LANES):
        table = table_ref[:, 2 * step * LANES : 2 * (step + 1) * LANES]
        whiten_bins(x, table, out_ref, slice(step * LANES, (step + 1) * LANES))


def hint(work):
    return pl.CostEstimate(flops=work, bytes_accessed=1 << 16, transcendentals=0)


def pinned(*arrays):
    return tuple(pltpu.with_memory_space_constraint(array, pltpu.VMEM) for array in arrays)


HERE = pl.BlockSpec(memory_space=pltpu.VMEM)


def whiten_first(x, parts):
    blocks, channels, samples = x.shape
    return pl.pallas_call(
        first_kernel,
        in_specs=[HERE, HERE, pl.BlockSpec(memory_space=pl.ANY)],
        out_specs=[HERE] * 3,
        out_shape=[
            pltpu.VMEM((samples, 2 * samples), jnp.bfloat16),
            pltpu.VMEM((blocks, 2 * channels, samples), jnp.bfloat16),
            pltpu.VMEM(x.shape, x.dtype),
        ],
        scratch_shapes=[pltpu.VMEM((samples, LANES), jnp.float32)] * 2 + [pltpu.SemaphoreType.DMA],
        compiler_params=pltpu.CompilerParams(vmem_limit_bytes=12 * MIB),
        cost_estimate=hint(blocks * channels * samples),
        name="table_and_own",
    )(*pinned(*parts), pltpu.with_memory_space_constraint(x, pltpu.HBM))


def whiten_next(x, table, name):
    blocks, channels, samples = x.shape
    return pl.pallas_call(
        whiten_all,
        in_specs=[HERE] * 2,
        out_specs=HERE,
        out_shape=pltpu.VMEM((blocks, 2 * channels, samples), jnp.bfloat16),
        compiler_params=pltpu.CompilerParams(vmem_limit_bytes=12 * MIB),
        cost_estimate=hint(17 * 10**9),
        name=name,
    )(*pinned(x, table))


def last_kernel(
    slots_ref, x_ref, table_ref, own_ref, sibling_ref, near_ref, passed_ref, out_ref, group_ref, window_ref, sems
):
    blocks, channels, samples = x_ref.shape
    parts = ((own_ref, 0), (sibling_ref, 1), (near_ref, 2), (passed_ref, 4))
    copies = [
        pltpu.make_async_copy(ref, window_ref.at[pl.ds(place * blocks, blocks)], sems.at[at])
        for at, (ref, place) in enumerate(parts)
    ]
    for copy in copies:
        copy.start()
    group_ref[0] = sum(
        (slots_ref[0, slot] >= 0).astype(jnp.int32) for slot in range(SLOTS_PER_GROUP, slots_ref.shape[1], SLOTS_PER_GROUP)
    )
    whiten_all(x_ref, table_ref, window_ref.at[pl.ds(3 * blocks, blocks)])
    for copy in copies:
        copy.wait()
    owner = lax.axis_index("chan")

    def place(block):
        block = jnp.where(block >= 0, block, owner * blocks)
        away = (lax.div(block, blocks) - owner) * (1 - 2 * lax.rem(owner, 2))
        return lax.rem(away + GROUPS, GROUPS) * blocks + lax.rem(block, blocks)

    def pairs(start):
        found = []
        for slot in range(start, start + SLOTS_PER_STEP):
            first, second = slots_ref[0, slot], slots_ref[1, slot]
            product = lax.dot_general(
                window_ref[place(first)],
                window_ref[place(second)],
                (((1,), (1,)), ((), ())),
                preferred_element_type=jnp.float32,
            )
            real = product[:channels, :channels] + product[channels:, channels:]
            imag = product[channels:, :channels] - product[:channels, channels:]
            live = jnp.where(first >= 0, 0.25, 0.0)
            both = jnp.concatenate([real, imag], axis=1) * live
            found.append(both.reshape(channels // 8, 8, 2 * channels))
        for pair in range(SLOTS_PER_STEP // 2):
            first, second = found[2 * pair], found[2 * pair + 1]
            row = lax.broadcasted_iota(jnp.int32, first.shape, 1)
            rows = slice(4 * start + 8 * pair, 4 * start + 8 * (pair + 1))
            out_ref[:, 0, rows] = jnp.where(row < 4, first, pltpu.roll(second, 4, 1))
            out_ref[:, 1, rows] = jnp.where(row < 4, pltpu.roll(first, 4, 1), second)

    pairs(0)
    for start in range(SLOTS_PER_STEP, slots_ref.shape[1], SLOTS_PER_STEP):
        pl.when(slots_ref[0, start] >= 0)(functools.partial(pairs, start))


def far_and_pairs(slots, x, table, own, sibling, near, passed):
    blocks, channels, samples = x.shape
    slot_count = slots.shape[0]
    return pl.pallas_call(
        last_kernel,
        in_specs=[pl.BlockSpec(memory_space=pltpu.SMEM)] + [HERE] * 6,
        out_specs=[HERE, pl.BlockSpec(memory_space=pltpu.SMEM)],
        scratch_shapes=[
            pltpu.VMEM((GROUPS * blocks, 2 * channels, samples), jnp.bfloat16),
            pltpu.SemaphoreType.DMA((4,)),
        ],
        out_shape=[
            pltpu.VMEM((channels // 8, 2, slot_count * 4, 2 * channels), jnp.float32),
            jax.ShapeDtypeStruct((1,), jnp.int32),
        ],
        compiler_params=pltpu.CompilerParams(vmem_limit_bytes=20 * MIB),
        cost_estimate=hint(slot_count * channels * samples),
        name="far_and_pairs",
    )(slots.T, *pinned(x, table, own, sibling, near, passed))


def after_transfer(x, work, *others):
    anywhere = pl.BlockSpec(memory_space=pl.ANY)
    return pl.pallas_call(
        lambda x_ref, *refs: None,
        in_specs=[anywhere] * (1 + len(others)),
        out_specs=anywhere,
        out_shape=jax.ShapeDtypeStruct(x.shape, x.dtype),
        input_output_aliases={0: 0},
        compiler_params=pltpu.CompilerParams(vmem_limit_bytes=MIB),
        cost_estimate=hint(work),
        name="far_arrived",
    )(x, *others)


def on_device(strain, pair_slots):
    x = strain[0]
    blocks, channels, samples = x.shape
    owners = lax.axis_size("chan")
    windows = lax.axis_size("tm")
    slot_count = pair_slots.shape[0]
    even = range(0, owners, 2)
    odd = range(1, owners, 2)
    sibling_pairs = [(i, i ^ 1) for i in range(owners)]
    inside = lambda pairs: [(source, target) for source, target in pairs if 0 <= source < owners]
    near_pairs = inside([(i + 2, i) for i in even] + [(i - 2, i) for i in odd])
    far_pairs = inside([(i - 2, i) for i in even] + [(i + 2, i) for i in odd])

    near = lax.ppermute(x, "chan", near_pairs)
    table, own, again = whiten_first(x, table_parts(samples))
    sibling = lax.ppermute(own, "chan", sibling_pairs)
    far = lax.ppermute(again, "chan", far_pairs)
    far = after_transfer(far, 100 * 10**9, sibling)
    near = whiten_next(near, table, "near")
    passed = lax.ppermute(near, "chan", sibling_pairs)
    products, group = far_and_pairs(pair_slots, far, table, own, sibling, near, passed)

    rows = channels // windows
    products = products.reshape(windows, slot_count * rows, 2 * channels)

    def summed(slots, products):
        sent = products[:, : slots * rows].astype(jnp.float16)
        arrived = lax.all_to_all(sent, "tm", 0, 0, tiled=True)
        total = jnp.sum(arrived.astype(jnp.float32), axis=0) * (4.0 / (samples * windows))
        return jnp.pad(total, ((0, (slot_count - slots) * rows), (0, 0)))

    total = lax.switch(
        group[0],
        [functools.partial(summed, slots) for slots in range(SLOTS_PER_GROUP, slot_count + 1, SLOTS_PER_GROUP)],
        products,
    )
    return jnp.transpose(total.reshape(slot_count, rows, 2 * channels), (1, 0, 2))


def solution(mesh):
    return jax.shard_map(
        on_device,
        mesh=mesh,
        in_specs=(P("tm", "chan", None, None), P("chan", None)),
        out_specs=P("tm", "chan", None),
        check_vma=False,
    )
```

```python
import functools
import math

import jax
import jax.numpy as jnp
from jax import lax
from jax.experimental import pallas as pl
from jax.experimental.pallas import tpu as pltpu
from jax.sharding import PartitionSpec as P

LANES = 128
ROWS_PERIOD = 16
SPLIT = 32
GROUPS = 5
SLOTS_PER_STEP = 4
SLOTS_PER_GROUP = 2
MIB = 1024 * 1024


def table_parts(samples):
    shape = (4 * SPLIT + samples // LANES * ROWS_PERIOD, LANES)
    row = lax.broadcasted_iota(jnp.int32, shape, 0)
    bin_low = lax.broadcasted_iota(jnp.int32, shape, 1) + 1
    part = row // SPLIT
    at = row % SPLIT
    step_row = row - 4 * SPLIT
    phases = jnp.where(
        part == 0,
        bin_low * at * SPLIT,
        jnp.where(
            part == 1,
            bin_low * at,
            jnp.where(
                part == 2,
                2 * SPLIT * at,
                jnp.where(part == 3, 2 * at, (step_row // ROWS_PERIOD) * (step_row % ROWS_PERIOD) * LANES),
            ),
        ),
    )
    angles = (phases % (2 * samples)).astype(jnp.float32) * (math.pi / samples)
    return jnp.cos(angles), jnp.sin(angles)


def whiten_bins(x, table, out_ref, bins):
    blocks, channels, samples = x.shape
    spectra = jnp.dot(x.reshape(blocks * channels, samples), table, preferred_element_type=jnp.float32)
    for block in range(blocks):
        part = spectra[block * channels : (block + 1) * channels]
        real, imag = part[:, :LANES], part[:, LANES:]
        power = jnp.sum(real * real + imag * imag, axis=0, keepdims=True) * (1.0 / channels)
        scale = 1.0 / jnp.sqrt(power + 1e-05)
        out_ref[block, :channels, bins] = (real * scale).astype(jnp.bfloat16)
        out_ref[block, channels:, bins] = (imag * scale).astype(jnp.bfloat16)


def first_kernel(cos_ref, sin_ref, x_ref, table_ref, out_ref, again_ref, low_cos_ref, low_sin_ref, sem):
    samples = x_ref.shape[2]
    fetch = pltpu.make_async_copy(x_ref, again_ref, sem)
    fetch.start()
    rows = lambda ref, part: ref[part * SPLIT : (part + 1) * SPLIT, :]
    for at in range(samples // SPLIT):
        high = lambda ref, part: ref[part * SPLIT + at : part * SPLIT + at + 1, :]
        taper = 0.5 - 0.5 * (high(cos_ref, 2) * rows(cos_ref, 3) - high(sin_ref, 2) * rows(sin_ref, 3))
        cos = high(cos_ref, 0) * rows(cos_ref, 1) - high(sin_ref, 0) * rows(sin_ref, 1)
        sin = high(sin_ref, 0) * rows(cos_ref, 1) + high(cos_ref, 0) * rows(sin_ref, 1)
        low_cos_ref[at * SPLIT : (at + 1) * SPLIT, :] = taper * cos
        low_sin_ref[at * SPLIT : (at + 1) * SPLIT, :] = taper * sin

    shape = (samples // ROWS_PERIOD, ROWS_PERIOD, LANES)
    for step in range(samples // LANES):
        low_cos = low_cos_ref[...].reshape(shape)
        low_sin = low_sin_ref[...].reshape(shape)
        step_rows = slice(4 * SPLIT + step * ROWS_PERIOD, 4 * SPLIT + (step + 1) * ROWS_PERIOD)
        step_cos = cos_ref[step_rows, :][None]
        step_sin = sin_ref[step_rows, :][None]
        real = low_cos * step_cos - low_sin * step_sin
        imag = -(low_sin * step_cos + low_cos * step_sin)
        columns = slice(2 * step * LANES, (2 * step + 1) * LANES)
        table_ref[:, columns] = real.reshape(samples, LANES).astype(jnp.bfloat16)
        columns = slice((2 * step + 1) * LANES, (2 * step + 2) * LANES)
        table_ref[:, columns] = imag.reshape(samples, LANES).astype(jnp.bfloat16)
    fetch.wait()
    whiten_all(again_ref, table_ref, out_ref)


def whiten_all(x_ref, table_ref, out_ref):
    x = x_ref[...]
    for step in range(x.shape[2] // LANES):
        table = table_ref[:, 2 * step * LANES : 2 * (step + 1) * LANES]
        whiten_bins(x, table, out_ref, slice(step * LANES, (step + 1) * LANES))


def hint(work):
    return pl.CostEstimate(flops=work, bytes_accessed=1 << 16, transcendentals=0)


def pinned(*arrays):
    return tuple(pltpu.with_memory_space_constraint(array, pltpu.VMEM) for array in arrays)


HERE = pl.BlockSpec(memory_space=pltpu.VMEM)


def whiten_first(x, parts):
    blocks, channels, samples = x.shape
    return pl.pallas_call(
        first_kernel,
        in_specs=[HERE, HERE, pl.BlockSpec(memory_space=pl.ANY)],
        out_specs=[HERE] * 3,
        out_shape=[
            pltpu.VMEM((samples, 2 * samples), jnp.bfloat16),
            pltpu.VMEM((blocks, 2 * channels, samples), jnp.bfloat16),
            pltpu.VMEM(x.shape, x.dtype),
        ],
        scratch_shapes=[pltpu.VMEM((samples, LANES), jnp.float32)] * 2 + [pltpu.SemaphoreType.DMA],
        compiler_params=pltpu.CompilerParams(vmem_limit_bytes=12 * MIB),
        cost_estimate=hint(blocks * channels * samples),
        name="table_and_own",
    )(*pinned(*parts), pltpu.with_memory_space_constraint(x, pltpu.HBM))


def whiten_next(x, table, name):
    blocks, channels, samples = x.shape
    return pl.pallas_call(
        whiten_all,
        in_specs=[HERE] * 2,
        out_specs=HERE,
        out_shape=pltpu.VMEM((blocks, 2 * channels, samples), jnp.bfloat16),
        compiler_params=pltpu.CompilerParams(vmem_limit_bytes=12 * MIB),
        cost_estimate=hint(17 * 10**9),
        name=name,
    )(*pinned(x, table))


def last_kernel(
    slots_ref, x_ref, table_ref, own_ref, sibling_ref, near_ref, passed_ref, out_ref, group_ref, window_ref, sems
):
    blocks, channels, samples = x_ref.shape
    parts = ((own_ref, 0), (sibling_ref, 1), (near_ref, 2), (passed_ref, 4))
    copies = [
        pltpu.make_async_copy(ref, window_ref.at[pl.ds(place * blocks, blocks)], sems.at[at])
        for at, (ref, place) in enumerate(parts)
    ]
    for copy in copies:
        copy.start()
    group_ref[0] = sum(
        (slots_ref[0, slot] >= 0).astype(jnp.int32) for slot in range(SLOTS_PER_GROUP, slots_ref.shape[1], SLOTS_PER_GROUP)
    )
    whiten_all(x_ref, table_ref, window_ref.at[pl.ds(3 * blocks, blocks)])
    for copy in copies:
        copy.wait()
    owner = lax.axis_index("chan")

    def place(block):
        block = jnp.where(block >= 0, block, owner * blocks)
        away = (lax.div(block, blocks) - owner) * (1 - 2 * lax.rem(owner, 2))
        return lax.rem(away + GROUPS, GROUPS) * blocks + lax.rem(block, blocks)

    def pairs(start):
        found = []
        for slot in range(start, start + SLOTS_PER_STEP):
            first, second = slots_ref[0, slot], slots_ref[1, slot]
            product = lax.dot_general(
                window_ref[place(first)],
                window_ref[place(second)],
                (((1,), (1,)), ((), ())),
                preferred_element_type=jnp.float32,
            )
            real = product[:channels, :channels] + product[channels:, channels:]
            imag = product[channels:, :channels] - product[:channels, channels:]
            live = jnp.where(first >= 0, 0.25, 0.0)
            both = jnp.concatenate([real, imag], axis=1) * live
            found.append(both.reshape(channels // 8, 8, 2 * channels))
        for pair in range(SLOTS_PER_STEP // 2):
            first, second = found[2 * pair], found[2 * pair + 1]
            row = lax.broadcasted_iota(jnp.int32, first.shape, 1)
            rows = slice(4 * start + 8 * pair, 4 * start + 8 * (pair + 1))
            out_ref[:, 0, rows] = jnp.where(row < 4, first, pltpu.roll(second, 4, 1))
            out_ref[:, 1, rows] = jnp.where(row < 4, pltpu.roll(first, 4, 1), second)

    pairs(0)
    for start in range(SLOTS_PER_STEP, slots_ref.shape[1], SLOTS_PER_STEP):
        pl.when(slots_ref[0, start] >= 0)(functools.partial(pairs, start))


def far_and_pairs(slots, x, table, own, sibling, near, passed):
    blocks, channels, samples = x.shape
    slot_count = slots.shape[0]
    return pl.pallas_call(
        last_kernel,
        in_specs=[pl.BlockSpec(memory_space=pltpu.SMEM)] + [HERE] * 6,
        out_specs=[HERE, pl.BlockSpec(memory_space=pltpu.SMEM)],
        scratch_shapes=[
            pltpu.VMEM((GROUPS * blocks, 2 * channels, samples), jnp.bfloat16),
            pltpu.SemaphoreType.DMA((4,)),
        ],
        out_shape=[
            pltpu.VMEM((channels // 8, 2, slot_count * 4, 2 * channels), jnp.float32),
            jax.ShapeDtypeStruct((1,), jnp.int32),
        ],
        compiler_params=pltpu.CompilerParams(vmem_limit_bytes=20 * MIB),
        cost_estimate=hint(slot_count * channels * samples),
        name="far_and_pairs",
    )(slots.T, *pinned(x, table, own, sibling, near, passed))


def after_transfer(x, work, *others):
    anywhere = pl.BlockSpec(memory_space=pl.ANY)
    return pl.pallas_call(
        lambda x_ref, *refs: None,
        in_specs=[anywhere] * (1 + len(others)),
        out_specs=anywhere,
        out_shape=jax.ShapeDtypeStruct(x.shape, x.dtype),
        input_output_aliases={0: 0},
        compiler_params=pltpu.CompilerParams(vmem_limit_bytes=MIB),
        cost_estimate=hint(work),
        name="far_arrived",
    )(x, *others)


def on_device(strain, pair_slots):
    x = strain[0]
    blocks, channels, samples = x.shape
    owners = lax.axis_size("chan")
    windows = lax.axis_size("tm")
    slot_count = pair_slots.shape[0]
    even = range(0, owners, 2)
    odd = range(1, owners, 2)
    sibling_pairs = [(i, i ^ 1) for i in range(owners)]
    inside = lambda pairs: [(source, target) for source, target in pairs if 0 <= source < owners]
    near_pairs = inside([(i + 2, i) for i in even] + [(i - 2, i) for i in odd])
    far_pairs = inside([(i - 2, i) for i in even] + [(i + 2, i) for i in odd])

    near = lax.ppermute(x, "chan", near_pairs)
    table, own, again = whiten_first(x, table_parts(samples))
    sibling = lax.ppermute(own, "chan", sibling_pairs)
    far = lax.ppermute(again, "chan", far_pairs)
    far = after_transfer(far, 100 * 10**9, sibling)
    near = whiten_next(near, table, "near")
    passed = lax.ppermute(near, "chan", sibling_pairs)
    products, group = far_and_pairs(pair_slots, far, table, own, sibling, near, passed)

    rows = channels // windows
    products = products.reshape(windows, slot_count * rows, 2 * channels)

    def summed(slots, products):
        sent = products[:, : slots * rows].astype(jnp.float16)
        arrived = lax.all_to_all(sent, "tm", 0, 0, tiled=True)
        total = jnp.sum(arrived.astype(jnp.float32) * (4.0 / (samples * windows)), axis=0)
        return jnp.pad(total, ((0, (slot_count - slots) * rows), (0, 0)))

    total = lax.switch(
        group[0],
        [functools.partial(summed, slots) for slots in range(SLOTS_PER_GROUP, slot_count + 1, SLOTS_PER_GROUP)],
        products,
    )
    return jnp.transpose(total.reshape(slot_count, rows, 2 * channels), (1, 0, 2))


def solution(mesh):
    return jax.shard_map(
        on_device,
        mesh=mesh,
        in_specs=(P("tm", "chan", None, None), P("chan", None)),
        out_specs=P("tm", "chan", None),
        check_vma=False,
    )
```

```python
import functools
import math

import jax
import jax.numpy as jnp
from jax import lax
from jax.experimental import pallas as pl
from jax.experimental.pallas import tpu as pltpu
from jax.sharding import PartitionSpec as P

LANES = 128
ROWS_PERIOD = 16
SPLIT = 32
GROUPS = 5
FEW_SLOTS = 6
SLOTS_PER_GROUP = 2
MIB = 1024 * 1024


def table_parts(samples):
    shape = (4 * SPLIT + samples // LANES * ROWS_PERIOD, LANES)
    row = lax.broadcasted_iota(jnp.int32, shape, 0)
    bin_low = lax.broadcasted_iota(jnp.int32, shape, 1) + 1
    part = row // SPLIT
    at = row % SPLIT
    step_row = row - 4 * SPLIT
    phases = jnp.where(
        part == 0,
        bin_low * at * SPLIT,
        jnp.where(
            part == 1,
            bin_low * at,
            jnp.where(
                part == 2,
                2 * SPLIT * at,
                jnp.where(part == 3, 2 * at, (step_row // ROWS_PERIOD) * (step_row % ROWS_PERIOD) * LANES),
            ),
        ),
    )
    angles = (phases % (2 * samples)).astype(jnp.float32) * (math.pi / samples)
    return jnp.cos(angles), jnp.sin(angles)


def whiten_bins(x, table, out_ref, bins):
    blocks, channels, samples = x.shape
    spectra = jnp.dot(x.reshape(blocks * channels, samples), table, preferred_element_type=jnp.float32)
    for block in range(blocks):
        part = spectra[block * channels : (block + 1) * channels]
        real, imag = part[:, :LANES], part[:, LANES:]
        power = jnp.sum(real * real + imag * imag, axis=0, keepdims=True) * (1.0 / channels)
        scale = 1.0 / jnp.sqrt(power + 1e-05)
        out_ref[block, :channels, bins] = (real * scale).astype(jnp.bfloat16)
        out_ref[block, channels:, bins] = (imag * scale).astype(jnp.bfloat16)


def first_kernel(cos_ref, sin_ref, x_ref, table_ref, out_ref, again_ref, low_cos_ref, low_sin_ref, sem):
    samples = x_ref.shape[2]
    fetch = pltpu.make_async_copy(x_ref, again_ref, sem)
    fetch.start()
    rows = lambda ref, part: ref[part * SPLIT : (part + 1) * SPLIT, :]
    for at in range(samples // SPLIT):
        high = lambda ref, part: ref[part * SPLIT + at : part * SPLIT + at + 1, :]
        taper = 0.5 - 0.5 * (high(cos_ref, 2) * rows(cos_ref, 3) - high(sin_ref, 2) * rows(sin_ref, 3))
        cos = high(cos_ref, 0) * rows(cos_ref, 1) - high(sin_ref, 0) * rows(sin_ref, 1)
        sin = high(sin_ref, 0) * rows(cos_ref, 1) + high(cos_ref, 0) * rows(sin_ref, 1)
        low_cos_ref[at * SPLIT : (at + 1) * SPLIT, :] = taper * cos
        low_sin_ref[at * SPLIT : (at + 1) * SPLIT, :] = taper * sin

    shape = (samples // ROWS_PERIOD, ROWS_PERIOD, LANES)
    for step in range(samples // LANES):
        low_cos = low_cos_ref[...].reshape(shape)
        low_sin = low_sin_ref[...].reshape(shape)
        step_rows = slice(4 * SPLIT + step * ROWS_PERIOD, 4 * SPLIT + (step + 1) * ROWS_PERIOD)
        step_cos = cos_ref[step_rows, :][None]
        step_sin = sin_ref[step_rows, :][None]
        real = low_cos * step_cos - low_sin * step_sin
        imag = -(low_sin * step_cos + low_cos * step_sin)
        columns = slice(2 * step * LANES, (2 * step + 1) * LANES)
        table_ref[:, columns] = real.reshape(samples, LANES).astype(jnp.bfloat16)
        columns = slice((2 * step + 1) * LANES, (2 * step + 2) * LANES)
        table_ref[:, columns] = imag.reshape(samples, LANES).astype(jnp.bfloat16)
    fetch.wait()
    whiten_all(again_ref, table_ref, out_ref)


def whiten_all(x_ref, table_ref, out_ref):
    x = x_ref[...]
    for step in range(x.shape[2] // LANES):
        table = table_ref[:, 2 * step * LANES : 2 * (step + 1) * LANES]
        whiten_bins(x, table, out_ref, slice(step * LANES, (step + 1) * LANES))


def hint(work):
    return pl.CostEstimate(flops=work, bytes_accessed=1 << 16, transcendentals=0)


def pinned(*arrays):
    return tuple(pltpu.with_memory_space_constraint(array, pltpu.VMEM) for array in arrays)


HERE = pl.BlockSpec(memory_space=pltpu.VMEM)


def whiten_first(x, parts):
    blocks, channels, samples = x.shape
    return pl.pallas_call(
        first_kernel,
        in_specs=[HERE, HERE, pl.BlockSpec(memory_space=pl.ANY)],
        out_specs=[HERE] * 3,
        out_shape=[
            pltpu.VMEM((samples, 2 * samples), jnp.bfloat16),
            pltpu.VMEM((blocks, 2 * channels, samples), jnp.bfloat16),
            pltpu.VMEM(x.shape, x.dtype),
        ],
        scratch_shapes=[pltpu.VMEM((samples, LANES), jnp.float32)] * 2 + [pltpu.SemaphoreType.DMA],
        compiler_params=pltpu.CompilerParams(vmem_limit_bytes=12 * MIB),
        cost_estimate=hint(blocks * channels * samples),
        name="table_and_own",
    )(*pinned(*parts), pltpu.with_memory_space_constraint(x, pltpu.HBM))


def whiten_next(x, table, name):
    blocks, channels, samples = x.shape
    return pl.pallas_call(
        whiten_all,
        in_specs=[HERE] * 2,
        out_specs=HERE,
        out_shape=pltpu.VMEM((blocks, 2 * channels, samples), jnp.bfloat16),
        compiler_params=pltpu.CompilerParams(vmem_limit_bytes=12 * MIB),
        cost_estimate=hint(17 * 10**9),
        name=name,
    )(*pinned(x, table))


def last_kernel(
    slots_ref, x_ref, table_ref, own_ref, sibling_ref, near_ref, passed_ref, out_ref, group_ref, window_ref, sems
):
    blocks, channels, samples = x_ref.shape
    parts = ((own_ref, 0), (sibling_ref, 1), (near_ref, 2), (passed_ref, 4))
    copies = [
        pltpu.make_async_copy(ref, window_ref.at[pl.ds(place * blocks, blocks)], sems.at[at])
        for at, (ref, place) in enumerate(parts)
    ]
    for copy in copies:
        copy.start()
    group_ref[0] = sum(
        (slots_ref[0, slot] >= 0).astype(jnp.int32) for slot in range(SLOTS_PER_GROUP, slots_ref.shape[1], SLOTS_PER_GROUP)
    )
    whiten_all(x_ref, table_ref, window_ref.at[pl.ds(3 * blocks, blocks)])
    for copy in copies:
        copy.wait()
    owner = lax.axis_index("chan")

    def place(block):
        block = jnp.where(block >= 0, block, owner * blocks)
        away = (lax.div(block, blocks) - owner) * (1 - 2 * lax.rem(owner, 2))
        return lax.rem(away + GROUPS, GROUPS) * blocks + lax.rem(block, blocks)

    def pairs(count):
        found = []
        for slot in range(count):
            first, second = slots_ref[0, slot], slots_ref[1, slot]
            product = lax.dot_general(
                window_ref[place(first)],
                window_ref[place(second)],
                (((1,), (1,)), ((), ())),
                preferred_element_type=jnp.float32,
            )
            real = product[:channels, :channels] + product[channels:, channels:]
            imag = product[channels:, :channels] - product[:channels, channels:]
            live = jnp.where(first >= 0, 0.25, 0.0)
            both = jnp.concatenate([real, imag], axis=1) * live
            found.append(both.reshape(channels // 8, 8, 2 * channels))
        for pair in range(count // 2):
            first, second = found[2 * pair], found[2 * pair + 1]
            row = lax.broadcasted_iota(jnp.int32, first.shape, 1)
            rows = slice(8 * pair, 8 * (pair + 1))
            out_ref[:, 0, rows] = jnp.where(row < 4, first, pltpu.roll(second, 4, 1))
            out_ref[:, 1, rows] = jnp.where(row < 4, pltpu.roll(first, 4, 1), second)

    many = slots_ref[0, FEW_SLOTS] >= 0
    pl.when(many)(functools.partial(pairs, slots_ref.shape[1]))
    pl.when(jnp.logical_not(many))(functools.partial(pairs, FEW_SLOTS))


def far_and_pairs(slots, x, table, own, sibling, near, passed):
    blocks, channels, samples = x.shape
    slot_count = slots.shape[0]
    return pl.pallas_call(
        last_kernel,
        in_specs=[pl.BlockSpec(memory_space=pltpu.SMEM)] + [HERE] * 6,
        out_specs=[HERE, pl.BlockSpec(memory_space=pltpu.SMEM)],
        scratch_shapes=[
            pltpu.VMEM((GROUPS * blocks, 2 * channels, samples), jnp.bfloat16),
            pltpu.SemaphoreType.DMA((4,)),
        ],
        out_shape=[
            pltpu.VMEM((channels // 8, 2, slot_count * 4, 2 * channels), jnp.float32),
            jax.ShapeDtypeStruct((1,), jnp.int32),
        ],
        compiler_params=pltpu.CompilerParams(vmem_limit_bytes=20 * MIB),
        cost_estimate=hint(slot_count * channels * samples),
        name="far_and_pairs",
    )(slots.T, *pinned(x, table, own, sibling, near, passed))


def after_transfer(x, work, *others):
    anywhere = pl.BlockSpec(memory_space=pl.ANY)
    return pl.pallas_call(
        lambda x_ref, *refs: None,
        in_specs=[anywhere] * (1 + len(others)),
        out_specs=anywhere,
        out_shape=jax.ShapeDtypeStruct(x.shape, x.dtype),
        input_output_aliases={0: 0},
        compiler_params=pltpu.CompilerParams(vmem_limit_bytes=MIB),
        cost_estimate=hint(work),
        name="far_arrived",
    )(x, *others)


def on_device(strain, pair_slots):
    x = strain[0]
    blocks, channels, samples = x.shape
    owners = lax.axis_size("chan")
    windows = lax.axis_size("tm")
    slot_count = pair_slots.shape[0]
    even = range(0, owners, 2)
    odd = range(1, owners, 2)
    sibling_pairs = [(i, i ^ 1) for i in range(owners)]
    inside = lambda pairs: [(source, target) for source, target in pairs if 0 <= source < owners]
    near_pairs = inside([(i + 2, i) for i in even] + [(i - 2, i) for i in odd])
    far_pairs = inside([(i - 2, i) for i in even] + [(i + 2, i) for i in odd])

    near = lax.ppermute(x, "chan", near_pairs)
    table, own, again = whiten_first(x, table_parts(samples))
    sibling = lax.ppermute(own, "chan", sibling_pairs)
    far = lax.ppermute(again, "chan", far_pairs)
    far = after_transfer(far, 100 * 10**9, sibling)
    near = whiten_next(near, table, "near")
    passed = lax.ppermute(near, "chan", sibling_pairs)
    products, group = far_and_pairs(pair_slots, far, table, own, sibling, near, passed)

    rows = channels // windows
    products = products.reshape(windows, slot_count * rows, 2 * channels)

    def summed(slots, products):
        sent = products[:, : slots * rows].astype(jnp.float16)
        arrived = lax.all_to_all(sent, "tm", 0, 0, tiled=True)
        total = jnp.sum(arrived.astype(jnp.float32), axis=0) * (4.0 / (samples * windows))
        return jnp.pad(total, ((0, (slot_count - slots) * rows), (0, 0)))

    total = lax.switch(
        group[0],
        [functools.partial(summed, slots) for slots in range(SLOTS_PER_GROUP, slot_count + 1, SLOTS_PER_GROUP)],
        products,
    )
    return jnp.transpose(total.reshape(slot_count, rows, 2 * channels), (1, 0, 2))


def solution(mesh):
    return jax.shard_map(
        on_device,
        mesh=mesh,
        in_specs=(P("tm", "chan", None, None), P("chan", None)),
        out_specs=P("tm", "chan", None),
        check_vma=False,
    )
```
